512 devices in a mesh: dp: 64 (over y, z), tensor: 8 (over x, core).
Axes of the slice: x: 4, y: 4, z: 16, core: 2. Of those that a mesh axis runs over, the one named last changes fastest.
Arguments:
- residual: bfloat16 [16384, 4096], P(('dp', 'tensor')), as said below
- context: bfloat16 [16384, 5120], P('dp', 'tensor'), may hold values from -6 to 6
- out_proj: bfloat16 [5120, 4096], P('tensor', 'dp'), may hold values from -0.078125 to 0.078125
- norm_gain: float32 [4096], replicated, may hold values from 0.1 to 1.9
- colbert_head: bfloat16 [4096, 128], P('tensor'), may hold values from -0.09375 to 0.09375
- candidates: int32 [512, 64], P(('dp', 'tensor')), may hold values from 0 to 4095, as said below
- lengths: int32 [4096], P('dp'), may hold values from 16 to 64, as said below
- centroid_ids: int32 [4096, 64], P('dp'), may hold values from 0 to 8191
- residual_codes: int32 [4096, 1024], P('dp'), may hold values from 0 to 65535
- centroids: bfloat16 [8192, 128], replicated, may hold values from -0.5 to 0.5
- buckets: float32 [4], replicated, may hold values from -0.1 to 0.1
Outputs:
- scores: float32 [512, 64], P(('dp', 'tensor'))
- context_grad: bfloat16 [16384, 5120], P('dp', 'tensor')
- residual_grad: bfloat16 [16384, 4096], P(('dp', 'tensor'))
- head_grad: float32 [4096, 128], P('tensor')
- gain_grad: float32 [4096], replicated
The draws below stay inside these ranges and needn't reach their ends.
Inputs may be any that keep to these rules, and one draw needn't show every extreme that they name: `candidates`: passage p lies in shard floor(p / 64). Of the 64 entries of one device's rows of dp+tensor, at most 2 name passages of one shard, and some shard has exactly 2 of them. Ids may repeat. `lengths`: each shard has a passage of exactly 64 tokens. `residual`: row scales and feature scales vary.
All inputs are finite; a program needn't handle non-finite values.
Results may differ from the reference program's by a relative error of at most 0.029.
Values may be sent and summed in bfloat16 or wider, within the bound.
No kernel may reach another device: no remote copies, remote signals or barrier semaphores. Data moves between devices by JAX's collectives and lax.ppermute only.
A program may use at most 128 MiB of HBM per device.

```python
import math
import jax
import jax.numpy as jnp
from jax import lax

D = 4096
INNER = 5120
DC = 128
QLEN = 32
NCAND = 64
DOCMAX = 64
NCENT = 8192
Q_LOC = 1
P_SHARD = 64
QUERIES = 512
TOKENS = 16384
NPASS = 4096
CAP = 2
WORDS = 16
N_DP = 64
N_TENSOR = 8


def draw_candidates(key, part):
    key = jax.random.fold_in(key, 11)
    block_count = N_DP * N_TENSOR
    slot_total = Q_LOC * NCAND
    owner_pool = jnp.arange(N_DP * CAP, dtype=jnp.int32) // CAP

    def one_block(block_key):
        key_one, key_two, key_three, key_four = jax.random.split(block_key, 4)
        chosen = jax.random.randint(key_one, (), 0, N_DP)
        ranking = jax.random.permutation(key_two, N_DP * CAP).astype(jnp.int32)
        ranking = jnp.where(owner_pool == chosen, -1 - ranking, ranking)
        arranged = jnp.argsort(ranking, stable=True)
        owner_list = jnp.take(owner_pool, arranged)[:slot_total]
        owner_list = jax.random.permutation(key_three, owner_list)
        local_list = jax.random.randint(key_four, (slot_total,), 0, P_SHARD)
        return (owner_list * P_SHARD + local_list).reshape(Q_LOC, NCAND)
    block_keys = jax.random.split(key, block_count)
    drawn = jax.vmap(one_block)(block_keys)
    return drawn.reshape(block_count * Q_LOC, NCAND).astype(jnp.int32)


def draw_lengths(key, part):
    key = jax.random.fold_in(key, 12)
    key_one, key_two = jax.random.split(key)
    base_len = jax.random.randint(key_one, (N_DP, P_SHARD), DOCMAX // 4, DOCMAX + 1)
    longest = jax.random.randint(key_two, (N_DP,), 0, P_SHARD)
    base_len = jnp.where(jnp.arange(P_SHARD)[None, :] == longest[:, None], DOCMAX, base_len)
    return base_len.reshape(N_DP * P_SHARD).astype(jnp.int32)


def draw_residual(key, part):
    key = jax.random.fold_in(key, 13)
    key_one, key_two, key_three = jax.random.split(key, 3)
    row_scale = jnp.exp(jax.random.uniform(key_one, (TOKENS, 1), jnp.float32, 0.0, math.log(10.0)))
    col_scale = jnp.exp(jax.random.uniform(key_two, (1, D), jnp.float32, 0.0, math.log(10.0)))
    base_vals = jax.random.normal(key_three, (TOKENS, D), jnp.float32)
    return (base_vals * row_scale * col_scale * 0.1).astype(jnp.bfloat16)


def place_ends(entries, stream_key, smallest, top_value):
    dims = entries.shape
    index_at = [jax.random.randint(jax.random.fold_in(stream_key, axis), (), 0, dims[axis]) for axis in range(len(dims))]
    entries = entries.at[tuple(index_at)].set(smallest)
    longest = dims.index(max(dims))
    index_at[longest] = (index_at[longest] + 1) % dims[longest]
    return entries.at[tuple(index_at)].set(top_value)


def shard_levels(key, extent, shards, least, top_value):
    def one(axis_at, shards_of):
        heights = jax.random.uniform(jax.random.fold_in(jax.random.fold_in(key, 6), axis_at), (shards_of,), jnp.float32, least / len(shards), top_value / len(shards))
        return jnp.repeat(jnp.exp(heights), extent[axis_at] // shards_of).reshape((-1,) + (1,) * (len(extent) - axis_at - 1))

    gain = one(*shards[0])
    for cut in shards[1:]:
        gain = gain * one(*cut)
    return gain


def centred(rng, shape, spread, most, cuts=(), kind=jnp.bfloat16):
    loudness = shard_levels(rng, shape, cuts, -0.22, 0.18) if cuts else 1.0
    values = jax.random.normal(rng, shape, jnp.float32) * spread * loudness
    return jnp.minimum(jnp.maximum(values, -most), most).astype(kind)


def setup_inputs(seed: int = 0) -> dict:
    seeds = jax.random.split(jax.random.key(seed), 12)
    return {
        "residual": draw_residual(jax.random.fold_in(seeds[11], 71), 0),
        "context": centred(seeds[1], (TOKENS, INNER), 1.0, 6.0, ((0, 64), (1, 8))),
        "out_proj": centred(seeds[2], (INNER, D), INNER ** -0.5, 0.078125, ((0, 8), (1, 64))),
        "norm_gain": jnp.clip(1.0 + 0.18 * jax.random.normal(seeds[3], (D,), jnp.float32), 0.1, 1.9),
        "colbert_head": centred(seeds[4], (D, DC), D ** -0.5, 0.09375, ((0, 8),)),
        "candidates": draw_candidates(jax.random.fold_in(seeds[11], 71), 0),
        "lengths": draw_lengths(jax.random.fold_in(seeds[11], 71), 0),
        "centroid_ids": place_ends(jax.random.randint(seeds[7], (NPASS, DOCMAX), 0, NCENT), jax.random.fold_in(seeds[7], 1), 0, NCENT - 1).astype(jnp.int32),
        "residual_codes": place_ends(jax.random.randint(seeds[8], (NPASS, DOCMAX * WORDS), 0, 65536), jax.random.fold_in(seeds[8], 1), 0, 65535).astype(jnp.int32),
        "centroids": centred(seeds[9], (NCENT, DC), DC ** -0.5, 0.5),
        "buckets": jnp.clip(jax.random.uniform(seeds[10], (4,), jnp.float32, -0.1, 0.1), -0.1, 0.1),
    }


EPS = 1e-06
TEMPER = 0.1
LOSS_SCALE = 64.0

def decompress(cell_ids, packed, centroids, buckets):
    leading = cell_ids.shape
    packed = packed.reshape(leading + (packed.shape[-1] // leading[-1], 1))
    shifts = 2 * jnp.arange(8, dtype=jnp.int32)
    code_vals = jnp.bitwise_and(jnp.right_shift(packed, shifts), 3)
    code_vals = code_vals.reshape(leading + (-1,))
    low_bit = jnp.bitwise_and(code_vals, 1).astype(jnp.float32)
    high_bit = jnp.right_shift(code_vals, 1).astype(jnp.float32)
    levels = buckets[0] + low_bit * (buckets[1] - buckets[0]) + high_bit * (buckets[2] - buckets[0]) + low_bit * high_bit * (buckets[3] - buckets[2] - buckets[1] + buckets[0])
    vectors = jnp.take(centroids, cell_ids, axis=0).astype(jnp.float32) + levels
    unit_scale = lax.rsqrt(lax.optimization_barrier(jnp.sum(vectors * vectors, axis=-1, keepdims=True)) + EPS)
    return (vectors * unit_scale).astype(jnp.bfloat16)

def soft_parts(similar, doc_spans):
    in_range = jnp.arange(similar.shape[-1])[None, None, :] < doc_spans[..., None, None]
    weights = jnp.where(in_range, jnp.exp(similar / TEMPER), 0.0)
    totals = lax.optimization_barrier(jnp.sum(weights, axis=-1))
    scores = TEMPER * lax.optimization_barrier(jnp.sum(jnp.log(totals), axis=-1))
    return (weights, totals, scores)

def seeds_of(scores):
    exponent = jnp.exp(scores)
    softmax_w = exponent / lax.optimization_barrier(jnp.sum(exponent, axis=-1, keepdims=True))
    positive = jnp.arange(scores.shape[-1]) == 0
    return LOSS_SCALE * (softmax_w - jnp.where(positive, 1.0, 0.0))

def reference(residual, context, out_proj, norm_gain, colbert_head, candidates, lengths, centroid_ids, residual_codes, centroids, buckets):
    head_span = INNER // N_TENSOR

    def add_part(total, shard_idx):
        start_at = (shard_idx * head_span).astype(jnp.int32)
        ctx_block = lax.dynamic_slice_in_dim(context, start_at, head_span, 1)
        out_rows = lax.dynamic_slice_in_dim(out_proj, start_at, head_span, 0)
        term = jnp.dot(ctx_block, out_rows, preferred_element_type=jnp.float32)
        return (total + lax.optimization_barrier(term.astype(jnp.bfloat16)).astype(jnp.float32), None)
    attended = lax.scan(add_part, jnp.zeros((TOKENS, D), jnp.float32), jnp.arange(N_TENSOR, dtype=jnp.int32))[0]
    summed = residual.astype(jnp.float32) + attended
    inv_rms = lax.rsqrt(lax.optimization_barrier(jnp.mean(summed * summed, axis=-1, keepdims=True)) + EPS)
    normed = (summed * inv_rms * norm_gain).astype(jnp.bfloat16)
    embedded = jnp.dot(normed, colbert_head, preferred_element_type=jnp.float32)
    inverse = lax.rsqrt(lax.optimization_barrier(jnp.sum(embedded * embedded, axis=-1, keepdims=True)) + EPS)
    queries = (embedded * inverse).astype(jnp.bfloat16)
    passages = decompress(centroid_ids, residual_codes, centroids, buckets)
    grouped = queries.reshape(QUERIES, QLEN, DC)

    def per_query(query_item):
        one_query, picked = query_item
        documents = jnp.take(passages, picked, axis=0)
        doc_spans = jnp.take(lengths, picked, axis=0)
        similar = jnp.einsum('id,ctd->cit', one_query.astype(jnp.float32), documents.astype(jnp.float32))
        weights, totals, scores = soft_parts(similar, doc_spans)
        score_seeds = seeds_of(scores)
        mixing = (score_seeds[:, None, None] * weights / totals[:, :, None]).astype(jnp.bfloat16)
        grad_query = jnp.einsum('cit,ctd->id', mixing.astype(jnp.float32), documents.astype(jnp.float32))
        return (scores, grad_query)
    scores, grad_queries = lax.map(per_query, (grouped, candidates))
    grad_q = grad_queries.reshape(TOKENS, DC)
    grad_embedded = (inverse * grad_q - inverse ** 3 * embedded * lax.optimization_barrier(jnp.sum(embedded * grad_q, axis=-1, keepdims=True))).astype(jnp.bfloat16)
    head_grad = jnp.dot(normed.T, grad_embedded, preferred_element_type=jnp.float32)
    grad_normed = jnp.dot(grad_embedded, colbert_head.T, preferred_element_type=jnp.float32)
    gain_grad = lax.optimization_barrier(jnp.sum(grad_normed * summed * inv_rms, axis=0))
    scaled = grad_normed * norm_gain
    residual_grad = (inv_rms * scaled - summed * inv_rms ** 3 * lax.optimization_barrier(jnp.mean(summed * scaled, axis=-1, keepdims=True))).astype(jnp.bfloat16)
    context_grad = jnp.dot(residual_grad, out_proj.T, preferred_element_type=jnp.float32).astype(jnp.bfloat16)
    return (scores, context_grad, residual_grad, head_grad, gain_grad)
```

```python
import jax
import jax.numpy as jnp
from jax import lax
from jax.sharding import Mesh, PartitionSpec as P

EPS = 1e-06
TEMPER = 0.1
LOSS_SCALE = 64.0

Y, Z, X, C = 4, 16, 4, 2
DP = ("y", "z")
TENSOR = ("x", "c")
PLANE = ("y", "x", "c")

BF16 = jnp.bfloat16
F32 = jnp.float32


def decode_all(cell_ids, packed, centroids, buckets):
    passages, tokens = cell_ids.shape
    words = packed.shape[1] // tokens
    features = centroids.shape[1]
    rows = passages * tokens
    packed = packed.reshape(rows, words)
    bytes_of = jnp.concatenate([packed & 255, (packed >> 8) & 255], axis=1).astype(BF16)
    feature = jnp.arange(features, dtype=jnp.int32)[None, :]
    source = jnp.arange(2 * words, dtype=jnp.int32)[:, None]
    spread = (source == (feature // 8) + words * ((feature % 8) // 4)).astype(BF16)
    code_bytes = jnp.dot(bytes_of, spread, preferred_element_type=F32).astype(jnp.int32)
    codes = (code_bytes >> (2 * (feature % 4))) & 3
    low = (codes & 1).astype(F32)
    high = (codes >> 1).astype(F32)
    levels = (
        buckets[0]
        + low * (buckets[1] - buckets[0])
        + high * (buckets[2] - buckets[0])
        + low * high * (buckets[3] - buckets[2] - buckets[1] + buckets[0])
    )
    vectors = jnp.take(centroids, cell_ids.reshape(rows), axis=0).astype(F32) + levels
    scale = lax.rsqrt(jnp.sum(vectors * vectors, axis=-1, keepdims=True) + EPS)
    return (vectors * scale).astype(BF16)


def halves(values):
    top = values.astype(BF16)
    return top, (values - top.astype(F32)).astype(BF16)


def local(
    residual,
    context,
    out_proj,
    norm_gain,
    colbert_head,
    candidates,
    lengths,
    centroid_ids,
    residual_codes,
    centroids,
    buckets,
):
    shards = Y * Z
    seq_rows, width = residual.shape
    cand_count = candidates.shape[1]
    per_shard, doc_len = centroid_ids.shape
    feature_dim = centroids.shape[1]
    cap = 2 * cand_count // shards
    slots = shards * cap

    slot_ids = candidates.reshape(-1)
    owners = slot_ids // per_shard
    local_ids = slot_ids - owners * per_shard
    order = jnp.arange(cand_count, dtype=jnp.int32)
    earlier = (owners[None, :] == owners[:, None]) & (order[None, :] < order[:, None])
    rank = jnp.sum(earlier.astype(jnp.int32), axis=1)
    position = owners * cap + rank
    placed = position[None, :] == jnp.arange(slots, dtype=jnp.int32)[:, None]
    request = jnp.sum(jnp.where(placed, local_ids[None, :], 0), axis=1).reshape(shards, cap)
    filled = jnp.any(placed, axis=1)
    note = jnp.concatenate(
        [
            jnp.broadcast_to(lengths[None, :], (shards, per_shard)),
            request,
            jnp.zeros((shards, 128 - per_shard - cap), jnp.int32),
        ],
        axis=1,
    )
    notes = lax.all_to_all(note, DP, 0, 0, tiled=True)

    proj_z = lax.all_gather(out_proj, "z", axis=1, tiled=True)
    context_y = lax.all_to_all(
        jnp.broadcast_to(context[None], (Y,) + context.shape), "y", 0, 0, tiled=True
    ).reshape(Y * context.shape[0], context.shape[1])

    documents = decode_all(centroid_ids, residual_codes, centroids, buckets)
    wanted = notes[:, per_shard : per_shard + cap].reshape(slots)
    chosen = jnp.take(documents.reshape(per_shard, doc_len, feature_dim), wanted, axis=0)
    got_docs = lax.all_to_all(
        chosen.reshape(shards, cap * doc_len, feature_dim), DP, 0, 0, tiled=True
    ).reshape(slots * doc_len, feature_dim)
    all_lengths = notes[:, None, :per_shard]
    spans = jnp.sum(
        jnp.where(
            jnp.arange(per_shard, dtype=jnp.int32)[None, None, :] == request[:, :, None],
            all_lengths,
            0,
        ),
        axis=2,
    ).reshape(slots)

    terms = jnp.dot(context_y, proj_z, preferred_element_type=F32).astype(BF16)
    parts = lax.all_to_all(terms, PLANE, 0, 0, tiled=True)
    parts = parts.reshape(Y, X * C, seq_rows, width // Y).astype(F32)
    attended = jnp.sum(parts, axis=1).transpose(1, 0, 2).reshape(seq_rows, width)
    summed = residual.astype(F32) + attended
    inv_rms = lax.rsqrt(jnp.mean(summed * summed, axis=-1, keepdims=True) + EPS)
    scaled_sum = summed * inv_rms
    normed = (scaled_sum * norm_gain).astype(BF16)

    proj_z_later, head_blk = lax.optimization_barrier((proj_z, colbert_head))
    head_full = lax.all_gather(head_blk, TENSOR, axis=0, tiled=True)
    proj_full = lax.all_gather(proj_z_later, "y", axis=1, tiled=True)
    unit_all = lax.all_gather(scaled_sum.astype(BF16), TENSOR, axis=0, tiled=True)

    embedded = jnp.dot(normed, head_full, preferred_element_type=F32)
    inverse = lax.rsqrt(jnp.sum(embedded * embedded, axis=-1, keepdims=True) + EPS)
    queries = (embedded * inverse).astype(BF16)

    similar = lax.dot_general(
        got_docs, queries, (((1,), (1,)), ((), ())), preferred_element_type=F32
    ).reshape(slots, doc_len, seq_rows)
    in_range = jnp.arange(doc_len, dtype=jnp.int32)[None, :, None] < spans[:, None, None]
    weights = jnp.where(in_range, jnp.exp(similar / TEMPER), 0.0)
    totals = jnp.sum(weights, axis=1)
    slot_scores = TEMPER * jnp.sum(jnp.log(totals), axis=-1)
    scores = jnp.sum(jnp.where(placed, slot_scores[:, None], 0.0), axis=0)[None, :]
    exponent = jnp.where(filled, jnp.exp(jnp.where(filled, slot_scores, 0.0)), 0.0)
    positive = jnp.arange(slots, dtype=jnp.int32) == position[0]
    seeds = LOSS_SCALE * (exponent / jnp.sum(exponent) - jnp.where(positive, 1.0, 0.0))
    mixing = (weights * (seeds[:, None] / totals)[:, None, :]).astype(BF16)
    grad_q = lax.dot_general(
        mixing.reshape(slots * doc_len, seq_rows),
        got_docs,
        (((0,), (0,)), ((), ())),
        preferred_element_type=F32,
    )

    along = jnp.sum(embedded * grad_q, axis=-1, keepdims=True)
    grad_embedded = (inverse * grad_q - inverse**3 * embedded * along).astype(BF16)
    pull = (
        inv_rms
        * jnp.sum(grad_embedded.astype(F32) * embedded, axis=-1, keepdims=True)
        * (1.0 / width)
    )
    packet = jnp.concatenate(
        [
            grad_embedded,
            *halves(pull),
            *halves(inv_rms),
            jnp.zeros((seq_rows, feature_dim - 4), BF16),
        ],
        axis=1,
    )
    packets = lax.all_gather(packet, TENSOR, axis=0, tiled=True)
    ge_all = packets[:, :feature_dim]
    extra = packets[:, feature_dim : feature_dim + 4].astype(F32)
    pull_all = extra[:, 0:1] + extra[:, 1:2]
    inv_all = extra[:, 2:3] + extra[:, 3:4]

    moments = lax.dot_general(
        unit_all, ge_all, (((0,), (0,)), ((), ())), preferred_element_type=F32
    )
    gain_term = jnp.sum(moments * head_full.astype(F32), axis=1).reshape(shards, width // shards)
    head_rows = colbert_head.shape[0]
    mine = (lax.axis_index("x") * C + lax.axis_index("c")) * head_rows
    head_term = lax.dynamic_slice_in_dim(moments, mine, head_rows, 0)
    share = head_rows // shards

    def bundle(head_part, gain_part):
        count = head_part.shape[0]
        return jnp.concatenate(
            [
                head_part.astype(BF16),
                jnp.concatenate(halves(gain_part), axis=1).reshape(count, 1, feature_dim),
                jnp.zeros((count, share - 1, feature_dim), BF16),
            ],
            axis=1,
        )

    def unbundle(rows):
        rows = rows.astype(F32)
        pair = rows[:, share]
        return rows[:, :share], pair[:, : width // shards] + pair[:, width // shards :]

    first = lax.all_to_all(
        bundle(head_term.reshape(shards, share, feature_dim), gain_term), DP, 0, 0, tiled=True
    )
    head_got, gain_got = unbundle(first)
    second = bundle(
        jnp.sum(head_got, axis=0, keepdims=True), jnp.sum(gain_got, axis=0, keepdims=True)
    )
    second = lax.all_to_all(
        jnp.broadcast_to(second, (shards,) + second.shape[1:]), DP, 0, 0, tiled=True
    )
    head_got, gain_got = unbundle(second)
    gain_blk = lax.dynamic_slice_in_dim(norm_gain, mine, head_rows, 0)
    head_grad = head_got.reshape(head_rows, feature_dim) * gain_blk[:, None]
    gain_grad = gain_got.reshape(width)

    grad_normed = lax.dot_general(
        grad_embedded, head_full, (((1,), (1,)), ((), ())), preferred_element_type=F32
    )
    scaled = grad_normed * norm_gain
    residual_grad = (
        inv_rms * scaled - summed * inv_rms**3 * jnp.mean(summed * scaled, axis=-1, keepdims=True)
    ).astype(BF16)
    gained_head = (head_full.astype(F32) * norm_gain[:, None]).astype(BF16)
    mixed_head = jnp.dot(proj_full, gained_head, preferred_element_type=F32).astype(BF16)
    pulled = lax.dot_general(
        unit_all, proj_full, (((1,), (1,)), ((), ())), preferred_element_type=F32
    )
    context_grad = (
        inv_all
        * lax.dot_general(
            ge_all, mixed_head, (((1,), (1,)), ((), ())), preferred_element_type=F32
        )
        - pull_all * pulled
    ).astype(BF16)
    return (scores, context_grad, residual_grad, head_grad, gain_grad)


def solution(mesh):
    split = Mesh(mesh.devices.reshape(Y, Z, X, C), ("y", "z", "x", "c"))
    both = DP + TENSOR
    in_specs = (
        P(both, None),
        P(DP, TENSOR),
        P(TENSOR, DP),
        P(),
        P(TENSOR, None),
        P(both, None),
        P(DP),
        P(DP, None),
        P(DP, None),
        P(),
        P(),
    )
    out_specs = (
        P(both, None),
        P(DP, TENSOR),
        P(both, None),
        P(TENSOR, None),
        P(),
    )
    return jax.shard_map(local, mesh=split, in_specs=in_specs, out_specs=out_specs, check_vma=False)
```

```python
import jax
import jax.numpy as jnp
from jax import lax
from jax.sharding import Mesh, PartitionSpec as P

EPS = 1e-06
TEMPER = 0.1
LOSS_SCALE = 64.0

Y, Z, X, C = 4, 16, 4, 2
DP = ("y", "z")
TENSOR = ("x", "c")
PLANE = ("y", "x", "c")

BF16 = jnp.bfloat16
F32 = jnp.float32


def decode_all(cell_ids, packed, centroids, buckets):
    passages, tokens = cell_ids.shape
    words = packed.shape[1] // tokens
    features = centroids.shape[1]
    rows = passages * tokens
    packed = packed.reshape(rows, words)
    bytes_of = jnp.concatenate([packed & 255, (packed >> 8) & 255], axis=1).astype(BF16)
    feature = jnp.arange(features, dtype=jnp.int32)[None, :]
    source = jnp.arange(2 * words, dtype=jnp.int32)[:, None]
    spread = (source == (feature // 8) + words * ((feature % 8) // 4)).astype(BF16)
    code_bytes = jnp.dot(bytes_of, spread, preferred_element_type=F32).astype(jnp.int32)
    codes = (code_bytes >> (2 * (feature % 4))) & 3
    low = (codes & 1).astype(F32)
    high = (codes >> 1).astype(F32)
    levels = (
        buckets[0]
        + low * (buckets[1] - buckets[0])
        + high * (buckets[2] - buckets[0])
        + low * high * (buckets[3] - buckets[2] - buckets[1] + buckets[0])
    )
    vectors = jnp.take(centroids, cell_ids.reshape(rows), axis=0).astype(F32) + levels
    scale = lax.rsqrt(jnp.sum(vectors * vectors, axis=-1, keepdims=True) + EPS)
    return (vectors * scale).astype(BF16)


def swap(values, axis, size, step):
    return lax.ppermute(values, axis, [(i, i ^ step) for i in range(size)])


def unxor(blocks, place):
    order = jnp.arange(blocks.shape[0], dtype=jnp.int32) ^ place
    return jnp.take(blocks, order, axis=0)


def halves(values):
    top = values.astype(BF16)
    return top, (values - top.astype(F32)).astype(BF16)


def local(
    residual,
    context,
    out_proj,
    norm_gain,
    colbert_head,
    candidates,
    lengths,
    centroid_ids,
    residual_codes,
    centroids,
    buckets,
):
    shards = Y * Z
    seq_rows, width = residual.shape
    cand_count = candidates.shape[1]
    per_shard, doc_len = centroid_ids.shape
    feature_dim = centroids.shape[1]
    cap = 2 * cand_count // shards
    slots = shards * cap

    slot_ids = candidates.reshape(-1)
    owners = slot_ids // per_shard
    local_ids = slot_ids - owners * per_shard
    order = jnp.arange(cand_count, dtype=jnp.int32)
    earlier = (owners[None, :] == owners[:, None]) & (order[None, :] < order[:, None])
    rank = jnp.sum(earlier.astype(jnp.int32), axis=1)
    position = owners * cap + rank
    placed = position[None, :] == jnp.arange(slots, dtype=jnp.int32)[:, None]
    request = jnp.sum(jnp.where(placed, local_ids[None, :], 0), axis=1).reshape(shards, cap)
    filled = jnp.any(placed, axis=1)
    note = jnp.concatenate(
        [
            jnp.broadcast_to(lengths[None, :], (shards, per_shard)),
            request,
            jnp.zeros((shards, 128 - per_shard - cap), jnp.int32),
        ],
        axis=1,
    )
    notes = lax.all_to_all(note, DP, 0, 0, tiled=True)

    proj_z = lax.all_gather(out_proj, "z", axis=1, tiled=True)
    documents = decode_all(centroid_ids, residual_codes, centroids, buckets)
    wanted = notes[:, per_shard : per_shard + cap].reshape(slots)
    chosen = jnp.take(documents.reshape(per_shard, doc_len, feature_dim), wanted, axis=0)
    chosen, context, colbert_head = lax.optimization_barrier((chosen, context, colbert_head))
    got_docs = lax.all_to_all(
        chosen.reshape(shards, cap * doc_len, feature_dim), DP, 0, 0, tiled=True
    ).reshape(slots * doc_len, feature_dim)
    all_lengths = notes[:, None, :per_shard]
    spans = jnp.sum(
        jnp.where(
            jnp.arange(per_shard, dtype=jnp.int32)[None, None, :] == request[:, :, None],
            all_lengths,
            0,
        ),
        axis=2,
    ).reshape(slots)

    here_x, here_c, here_y = lax.axis_index("x"), lax.axis_index("c"), lax.axis_index("y")
    blocks = context.reshape(X, C, seq_rows, context.shape[1])
    blocks = jnp.where(here_c == 0, blocks, blocks[:, ::-1])
    blocks = unxor(blocks, here_x).transpose(1, 0, 2, 3)
    by_y = jnp.stack([blocks] + [swap(blocks, "y", Y, step) for step in range(1, Y)], axis=2)
    by_y = by_y.reshape(C, X * Y * seq_rows, context.shape[1])

    head_pair = swap(colbert_head, "c", C, 1)
    head_pair = jnp.where(
        here_c == 0,
        jnp.stack([colbert_head, head_pair]),
        jnp.stack([head_pair, colbert_head]),
    )
    head_full = unxor(
        jnp.stack([head_pair] + [swap(head_pair, "x", X, step) for step in range(1, X)]), here_x
    ).reshape(width, feature_dim)

    by_y, head_full = lax.optimization_barrier((by_y, head_full))

    away = jnp.dot(by_y[1], proj_z, preferred_element_type=F32).astype(BF16)
    away = swap(away, "c", C, 1)
    stay = jnp.dot(by_y[0], proj_z, preferred_element_type=F32).astype(BF16)
    pair = (stay.astype(F32) + away.astype(F32)).reshape(X, Y, seq_rows, width // Y)
    for_x = pair.astype(BF16)
    row = pair[0]
    for step in range(1, X):
        row = row + swap(for_x[step], "x", X, step).astype(F32)
    for_y = row.astype(BF16)
    columns = [for_y[0]] + [swap(for_y[step], "y", Y, step) for step in range(1, Y)]
    columns = unxor(jnp.stack(columns), here_y)
    attended = columns.transpose(1, 0, 2).reshape(seq_rows, width).astype(F32)
    summed = residual.astype(F32) + attended
    inv_rms = lax.rsqrt(jnp.mean(summed * summed, axis=-1, keepdims=True) + EPS)
    scaled_sum = summed * inv_rms
    normed = (scaled_sum * norm_gain).astype(BF16)
    proj_full = lax.all_gather(proj_z, "y", axis=1, tiled=True)
    unit_all = lax.all_gather(scaled_sum.astype(BF16), TENSOR, axis=0, tiled=True)
    embedded = jnp.dot(normed, head_full, preferred_element_type=F32)
    inverse = lax.rsqrt(jnp.sum(embedded * embedded, axis=-1, keepdims=True) + EPS)
    queries = (embedded * inverse).astype(BF16)
    got_docs, unit_all = lax.optimization_barrier((got_docs, unit_all))

    similar = lax.dot_general(
        got_docs, queries, (((1,), (1,)), ((), ())), preferred_element_type=F32
    ).reshape(slots, doc_len, seq_rows)
    in_range = jnp.arange(doc_len, dtype=jnp.int32)[None, :, None] < spans[:, None, None]
    weights = jnp.where(in_range, jnp.exp(similar / TEMPER), 0.0)
    totals = jnp.sum(weights, axis=1)
    slot_scores = TEMPER * jnp.sum(jnp.log(totals), axis=-1)
    scores = jnp.sum(jnp.where(placed, slot_scores[:, None], 0.0), axis=0)[None, :]
    exponent = jnp.where(filled, jnp.exp(jnp.where(filled, slot_scores, 0.0)), 0.0)
    positive = jnp.arange(slots, dtype=jnp.int32) == position[0]
    seeds = LOSS_SCALE * (exponent / jnp.sum(exponent) - jnp.where(positive, 1.0, 0.0))
    mixing = (weights * (seeds[:, None] / totals)[:, None, :]).astype(BF16)
    grad_q = lax.dot_general(
        mixing.reshape(slots * doc_len, seq_rows),
        got_docs,
        (((0,), (0,)), ((), ())),
        preferred_element_type=F32,
    )

    along = jnp.sum(embedded * grad_q, axis=-1, keepdims=True)
    grad_embedded = (inverse * grad_q - inverse**3 * embedded * along).astype(BF16)
    pull = (
        inv_rms
        * jnp.sum(grad_embedded.astype(F32) * embedded, axis=-1, keepdims=True)
        * (1.0 / width)
    )
    packet = jnp.concatenate(
        [
            grad_embedded,
            *halves(pull),
            *halves(inv_rms),
            jnp.zeros((seq_rows, feature_dim - 4), BF16),
        ],
        axis=1,
    )
    packets = lax.all_to_all(
        jnp.broadcast_to(packet, (X * C,) + packet.shape), TENSOR, 0, 0, tiled=True
    ).reshape(X * C * seq_rows, 2 * feature_dim)
    ge_all = packets[:, :feature_dim]
    extra = packets[:, feature_dim : feature_dim + 4].astype(F32)
    pull_all = extra[:, 0:1] + extra[:, 1:2]
    inv_all = extra[:, 2:3] + extra[:, 3:4]

    moments = lax.dot_general(
        unit_all, ge_all, (((0,), (0,)), ((), ())), preferred_element_type=F32
    )
    gain_term = jnp.sum(moments * head_full.astype(F32), axis=1).reshape(shards, width // shards)
    head_rows = colbert_head.shape[0]
    mine = (lax.axis_index("x") * C + lax.axis_index("c")) * head_rows
    head_term = lax.dynamic_slice_in_dim(moments, mine, head_rows, 0)
    share = head_rows // shards

    def bundle(head_part, gain_part):
        count = head_part.shape[0]
        return jnp.concatenate(
            [
                head_part.astype(BF16),
                jnp.concatenate(halves(gain_part), axis=1).reshape(count, 1, feature_dim),
                jnp.zeros((count, share - 1, feature_dim), BF16),
            ],
            axis=1,
        )

    def unbundle(rows):
        rows = rows.astype(F32)
        pair = rows[..., share, :]
        return rows[..., :share, :], pair[..., : width // shards] + pair[..., width // shards :]

    rows = bundle(head_term.reshape(shards, share, feature_dim), gain_term)
    rows = lax.all_to_all(rows, "y", 0, 0, tiled=True)
    rows = unbundle(rows.reshape(Y, Z, 2 * share, feature_dim))
    rows = bundle(*[jnp.sum(part, axis=0) for part in rows])
    rows = unbundle(lax.all_to_all(rows, "z", 0, 0, tiled=True))
    rows = bundle(*[jnp.sum(part, axis=0, keepdims=True) for part in rows])
    rows = lax.all_to_all(
        jnp.broadcast_to(rows, (Z,) + rows.shape[1:]), "z", 0, 0, tiled=True
    )
    rows = lax.all_to_all(
        jnp.broadcast_to(rows[None], (Y,) + rows.shape), "y", 0, 0, tiled=True
    )
    head_got, gain_got = unbundle(rows.reshape(shards, 2 * share, feature_dim))
    gain_blk = lax.dynamic_slice_in_dim(norm_gain, mine, head_rows, 0)
    head_grad = head_got.reshape(head_rows, feature_dim) * gain_blk[:, None]
    gain_grad = gain_got.reshape(width)

    grad_normed = lax.dot_general(
        grad_embedded, head_full, (((1,), (1,)), ((), ())), preferred_element_type=F32
    )
    scaled = grad_normed * norm_gain
    residual_grad = (
        inv_rms * scaled - summed * inv_rms**3 * jnp.mean(summed * scaled, axis=-1, keepdims=True)
    ).astype(BF16)
    gained_head = (head_full.astype(F32) * norm_gain[:, None]).astype(BF16)
    mixed_head = jnp.dot(proj_full, gained_head, preferred_element_type=F32).astype(BF16)
    pulled = lax.dot_general(
        unit_all, proj_full, (((1,), (1,)), ((), ())), preferred_element_type=F32
    )
    context_grad = (
        inv_all
        * lax.dot_general(
            ge_all, mixed_head, (((1,), (1,)), ((), ())), preferred_element_type=F32
        )
        - pull_all * pulled
    ).astype(BF16)
    return (scores, context_grad, residual_grad, head_grad, gain_grad)


def solution(mesh):
    split = Mesh(mesh.devices.reshape(Y, Z, X, C), ("y", "z", "x", "c"))
    both = DP + TENSOR
    in_specs = (
        P(both, None),
        P(DP, TENSOR),
        P(TENSOR, DP),
        P(),
        P(TENSOR, None),
        P(both, None),
        P(DP),
        P(DP, None),
        P(DP, None),
        P(),
        P(),
    )
    out_specs = (
        P(both, None),
        P(DP, TENSOR),
        P(both, None),
        P(TENSOR, None),
        P(),
    )
    return jax.shard_map(local, mesh=split, in_specs=in_specs, out_specs=out_specs, check_vma=False)
```

```python
import jax
import jax.numpy as jnp
from jax import lax
from jax.experimental import pallas as pl
from jax.experimental.pallas import tpu as pltpu
from jax.sharding import Mesh, PartitionSpec as P

EPS = 1e-06
TEMPER = 0.1
LOSS_SCALE = 64.0

Y, Z, X, C = 4, 16, 4, 2
DP = ("y", "z")
TENSOR = ("x", "c")

BF16 = jnp.bfloat16
F32 = jnp.float32
I32 = jnp.int32
VMEM = pl.BlockSpec(memory_space=pltpu.VMEM)
SMEM = pl.BlockSpec(memory_space=pltpu.SMEM)


def swap(values, axis, size, step):
    return lax.ppermute(values, axis, [(i, i ^ step) for i in range(size)])


def rows_of(values, index):
    return values.at[index].get(mode="promise_in_bounds")


def unxor(blocks, place):
    return rows_of(blocks, jnp.arange(blocks.shape[0], dtype=I32) ^ place)


def halves(values):
    top = values.astype(BF16)
    return top, (values - top.astype(F32)).astype(BF16)


def decode_kernel(buckets, low_bytes, high_bytes, rows, out):
    words = low_bytes.shape[1]
    features = out.shape[1]
    feature = lax.broadcasted_iota(I32, (words, features), 1)
    word = lax.broadcasted_iota(I32, (words, features), 0)
    here = (feature >> 3) == word
    first = (feature & 7) < 4
    spread_low = jnp.where(here & first, 1.0, 0.0).astype(BF16)
    spread_high = jnp.where(here & ~first, 1.0, 0.0).astype(BF16)
    code_bytes = jnp.dot(low_bytes[...], spread_low, preferred_element_type=F32) + jnp.dot(
        high_bytes[...], spread_high, preferred_element_type=F32
    )
    shift = 2 * (lax.broadcasted_iota(I32, code_bytes.shape, 1) & 3)
    codes = (code_bytes.astype(I32) >> shift) & 3
    low = (codes & 1).astype(F32)
    high = (codes >> 1).astype(F32)
    zero, one, two, three = [buckets[k] for k in range(4)]
    levels = zero + low * (one - zero) + high * (two - zero)
    levels = levels + low * high * (three - two - one + zero)
    vectors = rows[...].astype(F32) + levels
    scale = lax.rsqrt(jnp.sum(vectors * vectors, axis=1, keepdims=True) + EPS)
    out[...] = (vectors * scale).astype(BF16)


def decode_all(cell_ids, packed, centroids, buckets):
    count = cell_ids.size
    words = packed.size // count
    features = centroids.shape[1]
    low_bytes = (packed & 255).astype(BF16).reshape(count, words)
    high_bytes = ((packed >> 8) & 255).astype(BF16).reshape(count, words)
    rows = rows_of(centroids, cell_ids.reshape(count))
    step = min(count, 512)
    return pl.pallas_call(
        decode_kernel,
        grid=(count // step,),
        in_specs=[
            SMEM,
            pl.BlockSpec((step, words), lambda i: (i, 0)),
            pl.BlockSpec((step, words), lambda i: (i, 0)),
            pl.BlockSpec((step, features), lambda i: (i, 0)),
        ],
        out_specs=pl.BlockSpec((step, features), lambda i: (i, 0)),
        out_shape=jax.ShapeDtypeStruct((count, features), BF16),
        name="decode",
    )(buckets, low_bytes, high_bytes, rows)


def score_kernel(docs_a, docs_b, embedded_ref, inv_rms_ref, spans, flags, scores, packet, weights, totals):
    slots, queries_n = totals.shape
    half = slots // 2
    tokens = docs_a.shape[0] // half
    features = docs_a.shape[1]
    embedded = embedded_ref[...]
    inv_rms = inv_rms_ref[...]
    inverse = lax.rsqrt(jnp.sum(embedded * embedded, axis=1, keepdims=True) + EPS)
    queries = (embedded * inverse).astype(BF16)
    group = 8
    token = lax.broadcasted_iota(I32, (tokens, queries_n), 0)

    for part, docs in enumerate((docs_a, docs_b)):

        @pl.loop(0, half // group)
        def _(i, part=part, docs=docs):
            at = pl.multiple_of(i * (group * tokens), group * tokens)
            slot0 = pl.multiple_of(part * half + i * group, group)
            similar = lax.dot_general(
                docs[pl.ds(at, group * tokens), :],
                queries,
                (((1,), (1,)), ((), ())),
                preferred_element_type=F32,
            )
            sizes = spans[pl.ds(slot0, group), :]
            sums = []
            for g in range(group):
                one = jnp.exp(similar[g * tokens : (g + 1) * tokens] / TEMPER)
                one = jnp.where(token < sizes[g : g + 1, :], one, 0.0)
                weights[pl.ds(slot0 * tokens + g * tokens, tokens), :] = one
                sums.append(jnp.sum(one, axis=0, keepdims=True))
            totals[pl.ds(slot0, group), :] = jnp.concatenate(sums, axis=0)

    all_totals = totals[...]
    slot_scores = TEMPER * jnp.sum(jnp.log(all_totals), axis=1, keepdims=True)
    scores[...] = slot_scores
    filled = flags[:, 0:1] > 0
    positive = flags[:, 1:2] > 0
    exponent = jnp.where(filled, jnp.exp(slot_scores), 0.0)
    share = exponent / jnp.sum(exponent, axis=0, keepdims=True)
    seeds = LOSS_SCALE * (share - jnp.where(positive, 1.0, 0.0))
    totals[...] = seeds / all_totals

    grad_q = jnp.zeros((queries_n, features), F32)
    for part, docs in enumerate((docs_a, docs_b)):

        def add(i, total, part=part, docs=docs):
            at = pl.multiple_of(i * (group * tokens), group * tokens)
            slot0 = pl.multiple_of(part * half + i * group, group)
            factors = totals[pl.ds(slot0, group), :]
            mixing = [
                weights[pl.ds(slot0 * tokens + g * tokens, tokens), :] * factors[g : g + 1, :]
                for g in range(group)
            ]
            mixing = jnp.concatenate(mixing, axis=0).astype(BF16)
            return total + lax.dot_general(
                mixing,
                docs[pl.ds(at, group * tokens), :],
                (((0,), (0,)), ((), ())),
                preferred_element_type=F32,
            )

        grad_q = lax.fori_loop(0, half // group, add, grad_q)

    along = jnp.sum(embedded * grad_q, axis=1, keepdims=True)
    grad_embedded = (inverse * grad_q - inverse * inverse * inverse * embedded * along).astype(BF16)
    packet[:, 0:features] = grad_embedded
    pull = inv_rms * jnp.sum(grad_embedded.astype(F32) * embedded, axis=1, keepdims=True)
    lane = lax.broadcasted_iota(I32, (queries_n, features), 1)
    extra = jnp.zeros((queries_n, features), F32)
    column = 0
    for value in (pull, inv_rms):
        for piece in halves(value):
            extra = jnp.where(lane == column, piece.astype(F32), extra)
            column += 1
    packet[:, features : 2 * features] = extra.astype(BF16)


def score(docs_a, docs_b, embedded, inv_rms, spans, flags):
    slots = flags.shape[0]
    queries_n, features = embedded.shape
    count = docs_a.shape[0] + docs_b.shape[0]
    return pl.pallas_call(
        score_kernel,
        in_specs=[VMEM] * 6,
        out_specs=[VMEM] * 2,
        out_shape=[
            jax.ShapeDtypeStruct((slots, 1), F32),
            jax.ShapeDtypeStruct((queries_n, 2 * features), BF16),
        ],
        scratch_shapes=[
            pltpu.VMEM((count, queries_n), F32),
            pltpu.VMEM((slots, queries_n), F32),
        ],
        compiler_params=pltpu.CompilerParams(vmem_limit_bytes=32 * 1024 * 1024),
        name="score",
    )(docs_a, docs_b, embedded, inv_rms, spans, flags)


def local(
    residual,
    context,
    out_proj,
    norm_gain,
    colbert_head,
    candidates,
    lengths,
    centroid_ids,
    residual_codes,
    centroids,
    buckets,
):
    shards = Y * Z
    seq_rows, width = residual.shape
    cand_count = candidates.shape[1]
    per_shard, doc_len = centroid_ids.shape
    feature_dim = centroids.shape[1]
    cap = 2
    slots = shards * cap

    slot_ids = candidates.reshape(-1)
    owners = slot_ids // per_shard
    local_ids = slot_ids - owners * per_shard
    order = jnp.arange(cand_count, dtype=I32)
    earlier = (owners[None, :] == owners[:, None]) & (order[None, :] < order[:, None])
    rank = jnp.sum(earlier.astype(I32), axis=1)
    position = rank * shards + owners
    slot_at = jnp.arange(slots, dtype=I32)
    placed = position[None, :] == slot_at[:, None]
    request = jnp.sum(jnp.where(placed, local_ids[None, :], 0), axis=1)
    filled = jnp.any(placed, axis=1)
    flags = jnp.stack([filled, slot_at == position[0]], axis=1).astype(I32)
    note = jnp.concatenate(
        [
            jnp.broadcast_to(lengths[None, :], (shards, per_shard)),
            request.reshape(cap, shards).T,
            jnp.zeros((shards, 128 - per_shard - cap), I32),
        ],
        axis=1,
    )

    proj_z = lax.all_gather(out_proj, "z", axis=1, tiled=True)
    documents = decode_all(centroid_ids, residual_codes, centroids, buckets)
    note, documents = lax.optimization_barrier((note, documents))
    notes = lax.all_to_all(note, DP, 0, 0, tiled=True)
    documents = documents.reshape(per_shard, doc_len, feature_dim)
    chosen_a = rows_of(documents, notes[:, per_shard])
    chosen_b = rows_of(documents, notes[:, per_shard + 1])
    chosen_a, chosen_b, context, colbert_head = lax.optimization_barrier(
        (chosen_a, chosen_b, context, colbert_head)
    )
    got_a = lax.all_to_all(chosen_a, DP, 0, 0, tiled=True).reshape(shards * doc_len, feature_dim)
    spans = jnp.sum(
        jnp.where(
            jnp.arange(per_shard, dtype=I32)[None, None, :]
            == request.reshape(cap, shards)[:, :, None],
            notes[None, :, :per_shard],
            0,
        ),
        axis=2,
    ).reshape(slots, 1)
    spans = jnp.broadcast_to(spans, (slots, seq_rows))

    here_x, here_c, here_y = lax.axis_index("x"), lax.axis_index("c"), lax.axis_index("y")
    blocks = context.reshape(X, C, seq_rows, context.shape[1])
    blocks = jnp.where(here_c == 0, blocks, blocks[:, ::-1])
    blocks = unxor(blocks, here_x).transpose(1, 0, 2, 3)
    by_y = jnp.stack([blocks] + [swap(blocks, "y", Y, step) for step in range(1, Y)], axis=2)
    by_y = by_y.reshape(C, X * Y * seq_rows, context.shape[1])

    head_pair = swap(colbert_head, "c", C, 1)
    head_pair = jnp.where(
        here_c == 0,
        jnp.stack([colbert_head, head_pair]),
        jnp.stack([head_pair, colbert_head]),
    )
    head_full = unxor(
        jnp.stack([head_pair] + [swap(head_pair, "x", X, step) for step in range(1, X)]), here_x
    ).reshape(width, feature_dim)
    by_y, head_full, got_a, proj_z = lax.optimization_barrier((by_y, head_full, got_a, proj_z))

    got_b = lax.all_to_all(chosen_b, DP, 0, 0, tiled=True).reshape(shards * doc_len, feature_dim)
    away = jnp.dot(by_y[1], proj_z, preferred_element_type=F32).astype(BF16)
    away = swap(away, "c", C, 1)
    stay = jnp.dot(by_y[0], proj_z, preferred_element_type=F32).astype(BF16)
    pair = (stay.astype(F32) + away.astype(F32)).reshape(X, Y, seq_rows, width // Y)
    for_x = pair.astype(BF16)
    row = pair[0]
    for step in range(1, X):
        row = row + swap(for_x[step], "x", X, step).astype(F32)
    for_y = row.astype(BF16)
    columns = [for_y[0]] + [swap(for_y[step], "y", Y, step) for step in range(1, Y)]
    columns = unxor(jnp.stack(columns), here_y)
    attended = columns.transpose(1, 0, 2).reshape(seq_rows, width).astype(F32)
    summed = residual.astype(F32) + attended
    inv_rms = lax.rsqrt(jnp.mean(summed * summed, axis=-1, keepdims=True) + EPS)
    scaled_sum = summed * inv_rms
    normed = (scaled_sum * norm_gain).astype(BF16)
    proj_full = lax.all_gather(proj_z, "y", axis=1, tiled=True)
    unit, proj_full = lax.optimization_barrier((scaled_sum.astype(BF16), proj_full))
    unit_all = lax.all_gather(unit, TENSOR, axis=0, tiled=True)
    embedded = jnp.dot(normed, head_full, preferred_element_type=F32)

    slot_scores, packet = score(got_a, got_b, embedded, inv_rms, spans, flags)
    scores = jnp.sum(jnp.where(placed, slot_scores, 0.0), axis=0)[None, :]
    packets = lax.all_to_all(
        jnp.broadcast_to(packet, (X * C,) + packet.shape), TENSOR, 0, 0, tiled=True
    ).reshape(X * C * seq_rows, 2 * feature_dim)
    ge_all = packets[:, :feature_dim]
    extra = packets[:, feature_dim : feature_dim + 4].astype(F32)
    pull_all = (extra[:, 0:1] + extra[:, 1:2]) * (1.0 / width)
    inv_all = extra[:, 2:3] + extra[:, 3:4]

    head_rows = colbert_head.shape[0]
    mine = (here_x * C + here_c) * head_rows
    head_term = lax.dot_general(
        lax.dynamic_slice_in_dim(unit_all, mine, head_rows, 1),
        ge_all,
        (((0,), (0,)), ((), ())),
        preferred_element_type=F32,
    )
    gain_term = jnp.sum(
        lax.dot_general(
            ge_all, head_full, (((1,), (1,)), ((), ())), preferred_element_type=F32
        )
        * unit_all.astype(F32),
        axis=0,
    )
    share = head_rows // shards
    lines = width // feature_dim

    def bundle(head_part, gain_part):
        return jnp.concatenate(
            [head_part.astype(BF16)] + [piece[:, None, :] for piece in halves(gain_part)], axis=1
        )

    def unbundle(rows):
        rows = rows.astype(F32)
        return rows[:, :share], rows[:, share] + rows[:, share + 1]

    gain_term = jnp.concatenate(
        [gain_term.reshape(lines, feature_dim), jnp.zeros((shards - lines, feature_dim), F32)]
    )
    first = bundle(head_term.reshape(shards, share, feature_dim), gain_term)
    first = unbundle(lax.all_to_all(first, DP, 0, 0, tiled=True))
    second = bundle(*[jnp.sum(part, axis=0, keepdims=True) for part in first])

    grad_embedded = packet[:, :feature_dim]
    grad_normed = lax.dot_general(
        grad_embedded, head_full, (((1,), (1,)), ((), ())), preferred_element_type=F32
    )
    scaled = grad_normed * norm_gain
    residual_grad = (
        inv_rms * scaled - summed * inv_rms**3 * jnp.mean(summed * scaled, axis=-1, keepdims=True)
    ).astype(BF16)
    gained_head = (head_full.astype(F32) * norm_gain[:, None]).astype(BF16)
    mixed_head = jnp.dot(proj_full, gained_head, preferred_element_type=F32).astype(BF16)
    pulled = lax.dot_general(
        unit_all, proj_full, (((1,), (1,)), ((), ())), preferred_element_type=F32
    )
    context_grad = (
        inv_all
        * lax.dot_general(
            ge_all, mixed_head, (((1,), (1,)), ((), ())), preferred_element_type=F32
        )
        - pull_all * pulled
    ).astype(BF16)
    second, context_grad = lax.optimization_barrier((second, context_grad))

    second = lax.all_to_all(
        jnp.broadcast_to(second, (shards,) + second.shape[1:]), DP, 0, 0, tiled=True
    )
    head_got, gain_got = unbundle(second)
    gain_blk = lax.dynamic_slice_in_dim(norm_gain, mine, head_rows, 0)
    head_grad = head_got.reshape(head_rows, feature_dim) * gain_blk[:, None]
    gain_grad = gain_got[:lines].reshape(width)
    return (scores, context_grad, residual_grad, head_grad, gain_grad)


def solution(mesh):
    split = Mesh(mesh.devices.reshape(Y, Z, X, C), ("y", "z", "x", "c"))
    both = DP + TENSOR
    in_specs = (
        P(both, None),
        P(DP, TENSOR),
        P(TENSOR, DP),
        P(),
        P(TENSOR, None),
        P(both, None),
        P(DP),
        P(DP, None),
        P(DP, None),
        P(),
        P(),
    )
    out_specs = (
        P(both, None),
        P(DP, TENSOR),
        P(both, None),
        P(TENSOR, None),
        P(),
    )
    return jax.shard_map(local, mesh=split, in_specs=in_specs, out_specs=out_specs, check_vma=False)
```

```python
import jax
import jax.numpy as jnp
from jax import lax
from jax.experimental import pallas as pl
from jax.experimental.pallas import tpu as pltpu
from jax.sharding import Mesh, PartitionSpec as P

EPS = 1e-06
TEMPER = 0.1
LOSS_SCALE = 64.0

Y, Z, X, C = 4, 16, 4, 2
DP = ("y", "z")
TENSOR = ("x", "c")

BF16 = jnp.bfloat16
F32 = jnp.float32
I32 = jnp.int32
VMEM = pl.BlockSpec(memory_space=pltpu.VMEM)
SMEM = pl.BlockSpec(memory_space=pltpu.SMEM)


def swap(values, axis, size, step):
    return lax.ppermute(values, axis, [(i, i ^ step) for i in range(size)])


def rows_of(values, index):
    return values.at[index].get(mode="promise_in_bounds")


def unxor(blocks, place):
    return rows_of(blocks, jnp.arange(blocks.shape[0], dtype=I32) ^ place)


def halves(values):
    top = values.astype(BF16)
    return top, (values - top.astype(F32)).astype(BF16)


def decode_kernel(buckets, low_bytes, high_bytes, rows, out):
    words = low_bytes.shape[1]
    features = out.shape[1]
    feature = lax.broadcasted_iota(I32, (words, features), 1)
    word = lax.broadcasted_iota(I32, (words, features), 0)
    here = (feature >> 3) == word
    first = (feature & 7) < 4
    spread_low = jnp.where(here & first, 1.0, 0.0).astype(BF16)
    spread_high = jnp.where(here & ~first, 1.0, 0.0).astype(BF16)
    code_bytes = jnp.dot(low_bytes[...], spread_low, preferred_element_type=F32) + jnp.dot(
        high_bytes[...], spread_high, preferred_element_type=F32
    )
    shift = 2 * (lax.broadcasted_iota(I32, code_bytes.shape, 1) & 3)
    codes = (code_bytes.astype(I32) >> shift) & 3
    low = (codes & 1).astype(F32)
    high = (codes >> 1).astype(F32)
    zero, one, two, three = [buckets[k] for k in range(4)]
    levels = zero + low * (one - zero) + high * (two - zero)
    levels = levels + low * high * (three - two - one + zero)
    vectors = rows[...].astype(F32) + levels
    scale = lax.rsqrt(jnp.sum(vectors * vectors, axis=1, keepdims=True) + EPS)
    out[...] = (vectors * scale).astype(BF16)


def decode_all(cell_ids, packed, centroids, buckets):
    count = cell_ids.size
    words = packed.size // count
    features = centroids.shape[1]
    low_bytes = (packed & 255).astype(BF16).reshape(count, words)
    high_bytes = ((packed >> 8) & 255).astype(BF16).reshape(count, words)
    rows = rows_of(centroids, cell_ids.reshape(count))
    step = min(count, 512)
    return pl.pallas_call(
        decode_kernel,
        grid=(count // step,),
        in_specs=[
            SMEM,
            pl.BlockSpec((step, words), lambda i: (i, 0)),
            pl.BlockSpec((step, words), lambda i: (i, 0)),
            pl.BlockSpec((step, features), lambda i: (i, 0)),
        ],
        out_specs=pl.BlockSpec((step, features), lambda i: (i, 0)),
        out_shape=jax.ShapeDtypeStruct((count, features), BF16),
        name="decode",
    )(buckets, low_bytes, high_bytes, rows)


def score_kernel(docs, embedded_ref, inv_rms_ref, spans, flags, scores, packet, weights, totals):
    slots, queries_n = totals.shape
    tokens = docs.shape[0] // slots
    features = docs.shape[1]
    embedded = embedded_ref[...]
    inv_rms = inv_rms_ref[...]
    inverse = lax.rsqrt(jnp.sum(embedded * embedded, axis=1, keepdims=True) + EPS)
    queries = (embedded * inverse).astype(BF16)
    group = 8
    token = lax.broadcasted_iota(I32, (tokens, queries_n), 0)

    @pl.loop(0, slots // group)
    def _(i):
        at = pl.multiple_of(i * (group * tokens), group * tokens)
        slot0 = pl.multiple_of(i * group, group)
        similar = lax.dot_general(
            docs[pl.ds(at, group * tokens), :],
            queries,
            (((1,), (1,)), ((), ())),
            preferred_element_type=F32,
        )
        sizes = spans[pl.ds(slot0, group), :]
        sums = []
        for g in range(group):
            one = jnp.exp(similar[g * tokens : (g + 1) * tokens] / TEMPER)
            one = jnp.where(token < sizes[g : g + 1, :], one, 0.0)
            weights[pl.ds(at + g * tokens, tokens), :] = one
            sums.append(jnp.sum(one, axis=0, keepdims=True))
        totals[pl.ds(slot0, group), :] = jnp.concatenate(sums, axis=0)

    all_totals = totals[...]
    slot_scores = TEMPER * jnp.sum(jnp.log(all_totals), axis=1, keepdims=True)
    scores[...] = slot_scores
    filled = flags[:, 0:1] > 0
    positive = flags[:, 1:2] > 0
    exponent = jnp.where(filled, jnp.exp(slot_scores), 0.0)
    share = exponent / jnp.sum(exponent, axis=0, keepdims=True)
    seeds = LOSS_SCALE * (share - jnp.where(positive, 1.0, 0.0))
    totals[...] = seeds / all_totals

    def add(i, total):
        at = pl.multiple_of(i * (group * tokens), group * tokens)
        slot0 = pl.multiple_of(i * group, group)
        factors = totals[pl.ds(slot0, group), :]
        mixing = [
            weights[pl.ds(at + g * tokens, tokens), :] * factors[g : g + 1, :]
            for g in range(group)
        ]
        mixing = jnp.concatenate(mixing, axis=0).astype(BF16)
        return total + lax.dot_general(
            mixing,
            docs[pl.ds(at, group * tokens), :],
            (((0,), (0,)), ((), ())),
            preferred_element_type=F32,
        )

    grad_q = lax.fori_loop(0, slots // group, add, jnp.zeros((queries_n, features), F32))
    along = jnp.sum(embedded * grad_q, axis=1, keepdims=True)
    grad_embedded = (inverse * grad_q - inverse * inverse * inverse * embedded * along).astype(BF16)
    packet[:, 0:features] = grad_embedded
    pull = inv_rms * jnp.sum(grad_embedded.astype(F32) * embedded, axis=1, keepdims=True)
    lane = lax.broadcasted_iota(I32, (queries_n, features), 1)
    extra = jnp.zeros((queries_n, features), F32)
    column = 0
    for value in (pull, inv_rms):
        for piece in halves(value):
            extra = jnp.where(lane == column, piece.astype(F32), extra)
            column += 1
    packet[:, features : 2 * features] = extra.astype(BF16)


def score(docs, embedded, inv_rms, spans, flags):
    slots = flags.shape[0]
    queries_n, features = embedded.shape
    count = docs.shape[0]
    return pl.pallas_call(
        score_kernel,
        in_specs=[VMEM] * 5,
        out_specs=[VMEM] * 2,
        out_shape=[
            jax.ShapeDtypeStruct((slots, 1), F32),
            jax.ShapeDtypeStruct((queries_n, 2 * features), BF16),
        ],
        scratch_shapes=[
            pltpu.VMEM((count, queries_n), F32),
            pltpu.VMEM((slots, queries_n), F32),
        ],
        compiler_params=pltpu.CompilerParams(vmem_limit_bytes=32 * 1024 * 1024),
        cost_estimate=pl.CostEstimate(
            flops=4 * count * queries_n * features,
            bytes_accessed=30_000_000,
            transcendentals=count * queries_n,
        ),
        name="score",
    )(docs, embedded, inv_rms, spans, flags)


def local(
    residual,
    context,
    out_proj,
    norm_gain,
    colbert_head,
    candidates,
    lengths,
    centroid_ids,
    residual_codes,
    centroids,
    buckets,
):
    shards = Y * Z
    seq_rows, width = residual.shape
    cand_count = candidates.shape[1]
    per_shard, doc_len = centroid_ids.shape
    feature_dim = centroids.shape[1]
    cap = 2
    slots = shards * cap

    slot_ids = candidates.reshape(-1)
    owners = slot_ids // per_shard
    local_ids = slot_ids - owners * per_shard
    order = jnp.arange(cand_count, dtype=I32)
    earlier = (owners[None, :] == owners[:, None]) & (order[None, :] < order[:, None])
    rank = jnp.sum(earlier.astype(I32), axis=1)
    position = owners * cap + rank
    slot_at = jnp.arange(slots, dtype=I32)
    placed = position[None, :] == slot_at[:, None]
    request = jnp.sum(jnp.where(placed, local_ids[None, :], 0), axis=1)
    filled = jnp.any(placed, axis=1)
    flags = jnp.stack([filled, slot_at == position[0]], axis=1).astype(I32)
    note = jnp.concatenate(
        [
            jnp.broadcast_to(lengths[None, :], (shards, per_shard)),
            request.reshape(shards, cap),
            jnp.zeros((shards, 128 - per_shard - cap), I32),
        ],
        axis=1,
    )

    proj_z = lax.all_gather(out_proj, "z", axis=1, tiled=True)
    documents = decode_all(centroid_ids, residual_codes, centroids, buckets)
    notes = lax.all_to_all(note, DP, 0, 0, tiled=True)
    documents = documents.reshape(per_shard, doc_len, feature_dim)
    chosen = rows_of(documents, notes[:, per_shard : per_shard + cap].reshape(slots))
    chosen, context, colbert_head = lax.optimization_barrier((chosen, context, colbert_head))
    got_docs = lax.all_to_all(
        chosen.reshape(shards, cap * doc_len, feature_dim), DP, 0, 0, tiled=True
    ).reshape(slots * doc_len, feature_dim)
    spans = jnp.sum(
        jnp.where(
            jnp.arange(per_shard, dtype=I32)[None, None, :]
            == request.reshape(shards, cap)[:, :, None],
            notes[:, None, :per_shard],
            0,
        ),
        axis=2,
    ).reshape(slots, 1)
    spans = jnp.broadcast_to(spans, (slots, seq_rows))

    here_x, here_c, here_y = lax.axis_index("x"), lax.axis_index("c"), lax.axis_index("y")
    blocks = context.reshape(X, C, seq_rows, context.shape[1])
    blocks = jnp.where(here_c == 0, blocks, blocks[:, ::-1])
    blocks = unxor(blocks, here_x).transpose(1, 0, 2, 3)
    by_y = jnp.stack([blocks] + [swap(blocks, "y", Y, step) for step in range(1, Y)], axis=2)
    by_y = by_y.reshape(C, X * Y * seq_rows, context.shape[1])

    head_pair = swap(colbert_head, "c", C, 1)
    head_pair = jnp.where(
        here_c == 0,
        jnp.stack([colbert_head, head_pair]),
        jnp.stack([head_pair, colbert_head]),
    )
    head_full = unxor(
        jnp.stack([head_pair] + [swap(head_pair, "x", X, step) for step in range(1, X)]), here_x
    ).reshape(width, feature_dim)
    by_y, head_full, proj_z = lax.optimization_barrier((by_y, head_full, proj_z))

    away = jnp.dot(by_y[1], proj_z, preferred_element_type=F32).astype(BF16)
    away = swap(away, "c", C, 1)
    stay = jnp.dot(by_y[0], proj_z, preferred_element_type=F32).astype(BF16)
    pair = (stay.astype(F32) + away.astype(F32)).reshape(X, Y, seq_rows, width // Y)
    pieces, row = [pair[step].astype(BF16) for step in range(1, X)], pair[0]
    for step in range(1, X):
        row = row + swap(pieces[step - 1], "x", X, step).astype(F32)
    for_y = row.astype(BF16)
    columns = [for_y[0]] + [swap(for_y[step], "y", Y, step) for step in range(1, Y)]
    columns = unxor(jnp.stack(columns), here_y)
    attended = columns.transpose(1, 0, 2).reshape(seq_rows, width).astype(F32)
    summed = residual.astype(F32) + attended
    inv_rms = lax.rsqrt(jnp.mean(summed * summed, axis=-1, keepdims=True) + EPS)
    scaled_sum = summed * inv_rms
    normed = (scaled_sum * norm_gain).astype(BF16)
    proj_full = lax.all_gather(proj_z, "y", axis=1, tiled=True)
    unit = scaled_sum.astype(BF16)
    unit = jnp.stack([unit, swap(unit, "c", C, 1)])
    units = [unit] + [swap(unit, "x", X, step) for step in range(1, X)]
    scaled_sum, normed, got_docs = lax.optimization_barrier((scaled_sum, normed, got_docs))
    embedded = jnp.dot(normed, head_full, preferred_element_type=F32)

    slot_scores, packet = score(got_docs, embedded, inv_rms, spans, flags)
    scores = jnp.sum(jnp.where(placed, slot_scores, 0.0), axis=0)[None, :]
    packet, units, proj_full = lax.optimization_barrier((packet, units, proj_full))
    unit_all = jnp.stack(units).reshape(X * C * seq_rows, width)
    packets = lax.all_to_all(
        jnp.broadcast_to(packet, (X * C,) + packet.shape), TENSOR, 0, 0, tiled=True
    )

    def reorder(rows):
        rows = rows.reshape(X * C, seq_rows, rows.shape[-1])
        return unxor(rows, here_x * C + here_c).reshape(X * C * seq_rows, rows.shape[-1])

    packets = reorder(packets)
    ge_all = packets[:, :feature_dim]
    extra = packets[:, feature_dim : feature_dim + 4].astype(F32)
    pull_all = (extra[:, 0:1] + extra[:, 1:2]) * (1.0 / width)
    inv_all = extra[:, 2:3] + extra[:, 3:4]

    head_rows = colbert_head.shape[0]
    mine = (here_x * C + here_c) * head_rows
    head_term = lax.dot_general(
        lax.dynamic_slice_in_dim(unit_all, mine, head_rows, 1),
        ge_all,
        (((0,), (0,)), ((), ())),
        preferred_element_type=F32,
    )
    gain_term = jnp.sum(
        lax.dot_general(
            ge_all, head_full, (((1,), (1,)), ((), ())), preferred_element_type=F32
        )
        * unit_all.astype(F32),
        axis=0,
    )
    share = head_rows // shards
    lines = width // feature_dim

    def bundle(head_part, gain_part):
        return jnp.concatenate(
            [head_part.astype(BF16)] + [piece[:, None, :] for piece in halves(gain_part)], axis=1
        )

    def unbundle(rows):
        pair = rows[:, share].astype(F32) + rows[:, share + 1].astype(F32)
        return rows[:, :share].astype(F32), pair

    gain_term = jnp.concatenate(
        [gain_term.reshape(lines, feature_dim), jnp.zeros((shards - lines, feature_dim), F32)]
    )
    first = bundle(head_term.reshape(shards, share, feature_dim), gain_term)
    first = unbundle(lax.all_to_all(first, DP, 0, 0, tiled=True))
    second = bundle(*[jnp.sum(part, axis=0, keepdims=True) for part in first])

    packet, packets = lax.optimization_barrier((packet, packets))
    grad_embedded = packet[:, :feature_dim]
    grad_normed = lax.dot_general(
        grad_embedded, head_full, (((1,), (1,)), ((), ())), preferred_element_type=F32
    )
    scaled = grad_normed * norm_gain
    residual_grad = (
        inv_rms * scaled - summed * inv_rms**3 * jnp.mean(summed * scaled, axis=-1, keepdims=True)
    ).astype(BF16)
    gained_head = (head_full.astype(F32) * norm_gain[:, None]).astype(BF16)
    mixed_head = jnp.dot(proj_full, gained_head, preferred_element_type=F32).astype(BF16)
    pulled = lax.dot_general(
        unit_all, proj_full, (((1,), (1,)), ((), ())), preferred_element_type=F32
    )
    context_grad = (
        inv_all
        * lax.dot_general(
            ge_all, mixed_head, (((1,), (1,)), ((), ())), preferred_element_type=F32
        )
        - pull_all * pulled
    ).astype(BF16)
    context_grad = reorder(context_grad)
    second, context_grad = lax.optimization_barrier((second, context_grad))

    second = lax.all_to_all(
        jnp.broadcast_to(second, (shards,) + second.shape[1:]), DP, 0, 0, tiled=True
    )
    head_got, gain_got = unbundle(second)
    gain_blk = lax.dynamic_slice_in_dim(norm_gain, mine, head_rows, 0)
    head_grad = head_got.reshape(head_rows, feature_dim) * gain_blk[:, None]
    gain_grad = gain_got[:lines].reshape(width)
    return (scores, context_grad, residual_grad, head_grad, gain_grad)


def solution(mesh):
    split = Mesh(mesh.devices.reshape(Y, Z, X, C), ("y", "z", "x", "c"))
    both = DP + TENSOR
    in_specs = (
        P(both, None),
        P(DP, TENSOR),
        P(TENSOR, DP),
        P(),
        P(TENSOR, None),
        P(both, None),
        P(DP),
        P(DP, None),
        P(DP, None),
        P(),
        P(),
    )
    out_specs = (
        P(both, None),
        P(DP, TENSOR),
        P(both, None),
        P(TENSOR, None),
        P(),
    )
    return jax.shard_map(local, mesh=split, in_specs=in_specs, out_specs=out_specs, check_vma=False)
```

```python
import jax
import jax.numpy as jnp
from jax import lax
from jax.experimental import pallas as pl
from jax.experimental.pallas import tpu as pltpu
from jax.sharding import Mesh, PartitionSpec as P

EPS = 1e-06
TEMPER = 0.1
LOSS_SCALE = 64.0

Y, Z, X, C = 4, 16, 4, 2
DP = ("y", "z")
TENSOR = ("x", "c")
PLANE = ("y", "x", "c")

BF16 = jnp.bfloat16
F32 = jnp.float32
I32 = jnp.int32
VMEM = pl.BlockSpec(memory_space=pltpu.VMEM)
SMEM = pl.BlockSpec(memory_space=pltpu.SMEM)


def swap(values, axis, size, step):
    return lax.ppermute(values, axis, [(i, i ^ step) for i in range(size)])


def rows_of(values, index):
    return values.at[index].get(mode="promise_in_bounds")


def unxor(blocks, place):
    return rows_of(blocks, jnp.arange(blocks.shape[0], dtype=I32) ^ place)


def decode_kernel(buckets, packed, rows, out):
    words = packed.shape[1]
    features = out.shape[1]
    feature = lax.broadcasted_iota(I32, (words, features), 1)
    word = lax.broadcasted_iota(I32, (words, features), 0)
    here = (feature >> 3) == word
    first = (feature & 7) < 4
    spread_low = jnp.where(here & first, 1.0, 0.0).astype(BF16)
    spread_high = jnp.where(here & ~first, 1.0, 0.0).astype(BF16)
    step = 256
    shift = 2 * (lax.broadcasted_iota(I32, (step, features), 1) & 3)
    zero, one, two, three = [buckets[k] for k in range(4)]

    @pl.loop(0, out.shape[0] // step)
    def _(i):
        at = pl.ds(pl.multiple_of(i * step, step), step)
        codes = packed[at, :]
        code_bytes = jnp.dot(
            (codes & 255).astype(F32).astype(BF16), spread_low, preferred_element_type=F32
        ) + jnp.dot(
            ((codes >> 8) & 255).astype(F32).astype(BF16), spread_high, preferred_element_type=F32
        )
        codes = (code_bytes.astype(I32) >> shift) & 3
        low = (codes & 1).astype(F32)
        high = (codes >> 1).astype(F32)
        levels = zero + low * (one - zero) + high * (two - zero)
        levels = levels + low * high * (three - two - one + zero)
        vectors = rows[at, :].astype(F32) + levels
        scale = lax.rsqrt(jnp.sum(vectors * vectors, axis=1, keepdims=True) + EPS)
        out[at, :] = (vectors * scale).astype(BF16)


def decode_all(cell_ids, packed, centroids, buckets):
    count = cell_ids.size
    packed = packed.reshape(count, packed.size // count)
    rows = rows_of(centroids, cell_ids.reshape(count))
    return pl.pallas_call(
        decode_kernel,
        in_specs=[SMEM, VMEM, VMEM],
        out_specs=VMEM,
        out_shape=jax.ShapeDtypeStruct((count, centroids.shape[1]), BF16),
        compiler_params=pltpu.CompilerParams(vmem_limit_bytes=32 * 1024 * 1024),
        name="decode",
    )(buckets, packed, rows)


def score_kernel(docs, embedded_ref, spans, flags, unit, head, scores, packet, weights, totals):
    slots, queries_n = totals.shape
    tokens = docs.shape[0] // slots
    features = docs.shape[1]
    embedded = embedded_ref[...]
    inverse = lax.rsqrt(jnp.sum(embedded * embedded, axis=1, keepdims=True) + EPS)
    queries = (embedded * inverse).astype(BF16)
    group = 8
    token = lax.broadcasted_iota(I32, (tokens, queries_n), 0)

    @pl.loop(0, slots // group)
    def _(i):
        at = pl.multiple_of(i * (group * tokens), group * tokens)
        slot0 = pl.multiple_of(i * group, group)
        similar = lax.dot_general(
            docs[pl.ds(at, group * tokens), :],
            queries,
            (((1,), (1,)), ((), ())),
            preferred_element_type=F32,
        )
        sizes = spans[pl.ds(slot0, group), :]
        sums = []
        for g in range(group):
            one = jnp.exp(similar[g * tokens : (g + 1) * tokens] / TEMPER)
            one = jnp.where(token < sizes[g : g + 1, :], one, 0.0)
            weights[pl.ds(at + g * tokens, tokens), :] = one
            sums.append(jnp.sum(one, axis=0, keepdims=True))
        totals[pl.ds(slot0, group), :] = jnp.concatenate(sums, axis=0)

    all_totals = totals[...]
    slot_scores = TEMPER * jnp.sum(jnp.log(all_totals), axis=1, keepdims=True)
    scores[...] = slot_scores
    filled = flags[:, 0:1] > 0
    positive = flags[:, 1:2] > 0
    exponent = jnp.where(filled, jnp.exp(slot_scores), 0.0)
    share = exponent / jnp.sum(exponent, axis=0, keepdims=True)
    seeds = LOSS_SCALE * (share - jnp.where(positive, 1.0, 0.0))
    totals[...] = seeds / all_totals

    def add(i, total):
        at = pl.multiple_of(i * (group * tokens), group * tokens)
        slot0 = pl.multiple_of(i * group, group)
        factors = totals[pl.ds(slot0, group), :]
        mixing = [
            weights[pl.ds(at + g * tokens, tokens), :] * factors[g : g + 1, :]
            for g in range(group)
        ]
        mixing = jnp.concatenate(mixing, axis=0).astype(BF16)
        return total + lax.dot_general(
            mixing,
            docs[pl.ds(at, group * tokens), :],
            (((0,), (0,)), ((), ())),
            preferred_element_type=F32,
        )

    grad_q = lax.fori_loop(0, slots // group, add, jnp.zeros((queries_n, features), F32))
    along = jnp.sum(embedded * grad_q, axis=1, keepdims=True)
    grad_embedded = (inverse * grad_q - inverse * inverse * inverse * embedded * along).astype(BF16)
    packet[0:queries_n, :] = grad_embedded

    block = 8
    for i in range(head.shape[0] // (block * features)):
        sums = []
        for k in range(i * block, (i + 1) * block):
            at = slice(k * features, (k + 1) * features)
            grad_normed = lax.dot_general(
                grad_embedded, head[at, :], (((1,), (1,)), ((), ())), preferred_element_type=F32
            )
            sums.append(jnp.sum(grad_normed * unit[:, at], axis=0, keepdims=True))
        line = queries_n + i * block
        packet[line : line + block, :] = jnp.concatenate(sums, axis=0).astype(BF16)


def score(docs, embedded, spans, flags, unit, head):
    slots = flags.shape[0]
    queries_n, features = embedded.shape
    count = docs.shape[0]
    return pl.pallas_call(
        score_kernel,
        in_specs=[VMEM] * 6,
        out_specs=[VMEM] * 2,
        out_shape=[
            jax.ShapeDtypeStruct((slots, 1), F32),
            jax.ShapeDtypeStruct((queries_n + head.shape[0] // features, features), BF16),
        ],
        scratch_shapes=[
            pltpu.VMEM((count, queries_n), F32),
            pltpu.VMEM((slots, queries_n), F32),
        ],
        compiler_params=pltpu.CompilerParams(vmem_limit_bytes=32 * 1024 * 1024),
        cost_estimate=pl.CostEstimate(
            flops=4 * count * queries_n * features,
            bytes_accessed=30_000_000,
            transcendentals=count * queries_n,
        ),
        name="score",
    )(docs, embedded, spans, flags, unit, head)


def local(
    residual,
    context,
    out_proj,
    norm_gain,
    colbert_head,
    candidates,
    lengths,
    centroid_ids,
    residual_codes,
    centroids,
    buckets,
):
    shards = Y * Z
    seq_rows, width = residual.shape
    cand_count = candidates.shape[1]
    per_shard, doc_len = centroid_ids.shape
    feature_dim = centroids.shape[1]
    cap = 2
    slots = shards * cap

    slot_ids = candidates.reshape(-1)
    owners = slot_ids // per_shard
    local_ids = slot_ids - owners * per_shard
    order = jnp.arange(cand_count, dtype=I32)
    earlier = (owners[None, :] == owners[:, None]) & (order[None, :] < order[:, None])
    rank = jnp.sum(earlier.astype(I32), axis=1)
    position = owners * cap + rank
    slot_at = jnp.arange(slots, dtype=I32)
    placed = position[None, :] == slot_at[:, None]
    request = jnp.sum(jnp.where(placed, local_ids[None, :], 0), axis=1)
    filled = jnp.any(placed, axis=1)
    flags = jnp.stack([filled, slot_at == position[0]], axis=1).astype(I32)
    note = jnp.concatenate(
        [
            jnp.broadcast_to(lengths[None, :], (shards, per_shard)),
            request.reshape(shards, cap),
            jnp.zeros((shards, 128 - per_shard - cap), I32),
        ],
        axis=1,
    )

    proj_z = lax.all_gather(out_proj, "z", axis=1, tiled=True)
    documents = decode_all(centroid_ids, residual_codes, centroids, buckets)
    notes = lax.all_to_all(note, DP, 0, 0, tiled=True)
    documents = documents.reshape(per_shard, doc_len, feature_dim)
    chosen = rows_of(documents, notes[:, per_shard : per_shard + cap].reshape(slots))
    chosen, context, colbert_head = lax.optimization_barrier((chosen, context, colbert_head))
    got_docs = lax.all_to_all(
        chosen.reshape(shards, cap * doc_len, feature_dim), DP, 0, 0, tiled=True
    ).reshape(slots * doc_len, feature_dim)
    spans = jnp.sum(
        jnp.where(
            jnp.arange(per_shard, dtype=I32)[None, None, :]
            == request.reshape(shards, cap)[:, :, None],
            notes[:, None, :per_shard],
            0,
        ),
        axis=2,
    ).reshape(slots, 1)
    spans = jnp.broadcast_to(spans, (slots, seq_rows))

    here_x, here_c, here_y = lax.axis_index("x"), lax.axis_index("c"), lax.axis_index("y")
    blocks = context.reshape(X, C, seq_rows, context.shape[1])
    blocks = jnp.where(here_c == 0, blocks, blocks[:, ::-1])
    blocks = unxor(blocks, here_x).transpose(1, 0, 2, 3)
    by_y = jnp.stack([blocks] + [swap(blocks, "y", Y, step) for step in range(1, Y)], axis=2)
    by_y = by_y.reshape(C, X * Y * seq_rows, context.shape[1])

    head_pair = swap(colbert_head, "c", C, 1)
    head_pair = jnp.where(
        here_c == 0,
        jnp.stack([colbert_head, head_pair]),
        jnp.stack([head_pair, colbert_head]),
    )
    head_full = unxor(
        jnp.stack([head_pair] + [swap(head_pair, "x", X, step) for step in range(1, X)]), here_x
    ).reshape(width, feature_dim)
    by_y, head_full, proj_z = lax.optimization_barrier((by_y, head_full, proj_z))

    away = jnp.dot(by_y[1], proj_z, preferred_element_type=F32).astype(BF16)
    away = swap(away, "c", C, 1)
    stay = jnp.dot(by_y[0], proj_z, preferred_element_type=F32).astype(BF16)
    stay = lax.optimization_barrier(stay)
    pair = (stay.astype(F32) + away.astype(F32)).reshape(X, Y, seq_rows, width // Y)
    pieces, row = [pair[step].astype(BF16) for step in range(1, X)], pair[0]
    for step in range(1, X):
        row = row + swap(pieces[step - 1], "x", X, step).astype(F32)
    for_y = row.astype(BF16)
    columns = [for_y[0]] + [swap(for_y[step], "y", Y, step) for step in range(1, Y)]
    columns = unxor(jnp.stack(columns), here_y)
    attended = columns.transpose(1, 0, 2).reshape(seq_rows, width).astype(F32)
    summed = residual.astype(F32) + attended
    inv_rms = lax.rsqrt(jnp.mean(summed * summed, axis=-1, keepdims=True) + EPS)
    scaled_sum = summed * inv_rms
    normed = (scaled_sum * norm_gain).astype(BF16)
    embedded = jnp.dot(normed, head_full, preferred_element_type=F32)

    head_rows = colbert_head.shape[0]
    unit = scaled_sum.astype(BF16).reshape(seq_rows, X * C, head_rows).transpose(1, 0, 2)
    unit, got_docs = lax.optimization_barrier((unit, got_docs))
    unit_plane = lax.all_to_all(
        jnp.concatenate([unit] * Y), PLANE, 0, 0, tiled=True
    ).reshape(Y * X * C * seq_rows, head_rows)

    slot_scores, packet = score(got_docs, embedded, spans, flags, scaled_sum, head_full)
    scores = jnp.sum(jnp.where(placed, slot_scores, 0.0), axis=0)[None, :]
    packet, unit_plane = lax.optimization_barrier((packet, unit_plane))
    packets = lax.all_to_all(
        jnp.broadcast_to(packet, (Y * X * C,) + packet.shape), PLANE, 0, 0, tiled=True
    )
    ge_plane = packets[:, :seq_rows]

    proj_full = lax.all_gather(proj_z, "y", axis=1, tiled=True)
    packets, summed_all, proj_full = lax.optimization_barrier(
        (packets, summed.astype(BF16), proj_full)
    )
    summed_all = lax.all_gather(summed_all, TENSOR, axis=0, tiled=True)

    share = head_rows // Z
    lines = width // feature_dim // Z
    head_term = lax.dot_general(
        unit_plane,
        ge_plane.reshape(Y * X * C * seq_rows, feature_dim),
        (((0,), (0,)), ((), ())),
        preferred_element_type=F32,
    )
    gain_term = jnp.sum(packets[:, seq_rows:].astype(F32), axis=0)
    first = jnp.concatenate(
        [
            head_term.reshape(Z, share, feature_dim).astype(BF16),
            gain_term.reshape(Z, lines, feature_dim).astype(BF16),
        ],
        axis=1,
    )
    first = lax.all_to_all(first, "z", 0, 0, tiled=True)
    second = jnp.sum(first.astype(F32), axis=0, keepdims=True).astype(BF16)
    second = lax.all_to_all(
        jnp.broadcast_to(second, (Z,) + second.shape[1:]), "z", 0, 0, tiled=True
    )

    packet, packets = lax.optimization_barrier((packet, packets))
    grad_embedded = packet[:seq_rows]
    grad_normed = lax.dot_general(
        grad_embedded, head_full, (((1,), (1,)), ((), ())), preferred_element_type=F32
    )
    scaled = grad_normed * norm_gain
    residual_grad = (
        inv_rms * scaled - summed * inv_rms**3 * jnp.mean(summed * scaled, axis=-1, keepdims=True)
    ).astype(BF16)
    ge_all = lax.dynamic_slice_in_dim(ge_plane, here_y * (X * C), X * C, 0)
    ge_all = ge_all.reshape(X * C * seq_rows, feature_dim)
    gained_head = (head_full.astype(F32) * norm_gain[:, None]).astype(BF16)
    mixed_head = jnp.dot(proj_full, gained_head, preferred_element_type=F32).astype(BF16)
    pulled = lax.dot_general(
        summed_all, proj_full, (((1,), (1,)), ((), ())), preferred_element_type=F32
    )
    wide = summed_all.astype(F32)
    inv_all = lax.rsqrt(jnp.mean(wide * wide, axis=-1, keepdims=True) + EPS)
    embedded_all = jnp.dot(summed_all, gained_head, preferred_element_type=F32)
    pull_all = jnp.sum(ge_all.astype(F32) * embedded_all, axis=-1, keepdims=True) * (1.0 / width)
    context_grad = (
        inv_all
        * lax.dot_general(
            ge_all, mixed_head, (((1,), (1,)), ((), ())), preferred_element_type=F32
        )
        - inv_all**3 * pull_all * pulled
    ).astype(BF16)

    second, context_grad = lax.optimization_barrier((second, context_grad))
    mine = (here_x * C + here_c) * head_rows
    gain_blk = lax.dynamic_slice_in_dim(norm_gain, mine, head_rows, 0)
    head_grad = second[:, :share].astype(F32).reshape(head_rows, feature_dim) * gain_blk[:, None]
    gain_grad = second[:, share:].astype(F32).reshape(width)
    return (scores, context_grad, residual_grad, head_grad, gain_grad)


def solution(mesh):
    split = Mesh(mesh.devices.reshape(Y, Z, X, C), ("y", "z", "x", "c"))
    both = DP + TENSOR
    in_specs = (
        P(both, None),
        P(DP, TENSOR),
        P(TENSOR, DP),
        P(),
        P(TENSOR, None),
        P(both, None),
        P(DP),
        P(DP, None),
        P(DP, None),
        P(),
        P(),
    )
    out_specs = (
        P(both, None),
        P(DP, TENSOR),
        P(both, None),
        P(TENSOR, None),
        P(),
    )
    return jax.shard_map(local, mesh=split, in_specs=in_specs, out_specs=out_specs, check_vma=False)
```

```python
import jax
import jax.numpy as jnp
from jax import lax
from jax.experimental import pallas as pl
from jax.experimental.pallas import tpu as pltpu
from jax.sharding import Mesh, PartitionSpec as P

EPS = 1e-06
TEMPER = 0.1
LOSS_SCALE = 64.0

Y, Z, X, C = 4, 16, 4, 2
DP = ("y", "z")
TENSOR = ("x", "c")
PLANE = ("y", "x", "c")

BF16 = jnp.bfloat16
F32 = jnp.float32
I32 = jnp.int32
VMEM = pl.BlockSpec(memory_space=pltpu.VMEM)
SMEM = pl.BlockSpec(memory_space=pltpu.SMEM)


def swap(values, axis, size, step):
    return lax.ppermute(values, axis, [(i, i ^ step) for i in range(size)])


def rows_of(values, index):
    return values.at[index].get(mode="promise_in_bounds")


def unxor(blocks, place):
    return rows_of(blocks, jnp.arange(blocks.shape[0], dtype=I32) ^ place)


def decode_kernel(buckets, packed, rows, out):
    words = packed.shape[1]
    features = out.shape[1]
    feature = lax.broadcasted_iota(I32, (words, features), 1)
    word = lax.broadcasted_iota(I32, (words, features), 0)
    here = (feature >> 3) == word
    first = (feature & 7) < 4
    spread_low = jnp.where(here & first, 1.0, 0.0).astype(BF16)
    spread_high = jnp.where(here & ~first, 1.0, 0.0).astype(BF16)
    step = 256
    shift = 2 * (lax.broadcasted_iota(I32, (step, features), 1) & 3)
    zero, one, two, three = [buckets[k] for k in range(4)]

    @pl.loop(0, out.shape[0] // step)
    def _(i):
        at = pl.ds(pl.multiple_of(i * step, step), step)
        codes = packed[at, :]
        code_bytes = jnp.dot(
            (codes & 255).astype(F32).astype(BF16), spread_low, preferred_element_type=F32
        ) + jnp.dot(
            ((codes >> 8) & 255).astype(F32).astype(BF16), spread_high, preferred_element_type=F32
        )
        codes = (code_bytes.astype(I32) >> shift) & 3
        low = (codes & 1).astype(F32)
        high = (codes >> 1).astype(F32)
        levels = zero + low * (one - zero) + high * (two - zero)
        levels = levels + low * high * (three - two - one + zero)
        vectors = rows[at, :].astype(F32) + levels
        scale = lax.rsqrt(jnp.sum(vectors * vectors, axis=1, keepdims=True) + EPS)
        out[at, :] = (vectors * scale).astype(BF16)


def decode_all(cell_ids, packed, centroids, buckets):
    count = cell_ids.size
    packed = packed.reshape(count, packed.size // count)
    rows = rows_of(centroids, cell_ids.reshape(count))
    return pl.pallas_call(
        decode_kernel,
        in_specs=[SMEM, VMEM, VMEM],
        out_specs=VMEM,
        out_shape=jax.ShapeDtypeStruct((count, centroids.shape[1]), BF16),
        compiler_params=pltpu.CompilerParams(vmem_limit_bytes=32 * 1024 * 1024),
        name="decode",
    )(buckets, packed, rows)


def score_kernel(docs, embedded_ref, spans, flags, unit, head, scores, packet, weights, totals):
    slots, queries_n = totals.shape
    tokens = docs.shape[0] // slots
    features = docs.shape[1]
    embedded = embedded_ref[...]
    inverse = lax.rsqrt(jnp.sum(embedded * embedded, axis=1, keepdims=True) + EPS)
    queries = (embedded * inverse).astype(BF16)
    group = 8
    token = lax.broadcasted_iota(I32, (tokens, queries_n), 0)

    @pl.loop(0, slots // group)
    def _(i):
        at = pl.multiple_of(i * (group * tokens), group * tokens)
        slot0 = pl.multiple_of(i * group, group)
        similar = lax.dot_general(
            docs[pl.ds(at, group * tokens), :],
            queries,
            (((1,), (1,)), ((), ())),
            preferred_element_type=F32,
        )
        sizes = spans[pl.ds(slot0, group), :]
        sums = []
        for g in range(group):
            one = jnp.exp(similar[g * tokens : (g + 1) * tokens] / TEMPER)
            one = jnp.where(token < sizes[g : g + 1, :], one, 0.0)
            weights[pl.ds(at + g * tokens, tokens), :] = one
            sums.append(jnp.sum(one, axis=0, keepdims=True))
        totals[pl.ds(slot0, group), :] = jnp.concatenate(sums, axis=0)

    all_totals = totals[...]
    slot_scores = TEMPER * jnp.sum(jnp.log(all_totals), axis=1, keepdims=True)
    scores[...] = slot_scores
    filled = flags[:, 0:1] > 0
    positive = flags[:, 1:2] > 0
    exponent = jnp.where(filled, jnp.exp(slot_scores), 0.0)
    share = exponent / jnp.sum(exponent, axis=0, keepdims=True)
    seeds = LOSS_SCALE * (share - jnp.where(positive, 1.0, 0.0))
    totals[...] = seeds / all_totals

    def add(i, total):
        at = pl.multiple_of(i * (group * tokens), group * tokens)
        slot0 = pl.multiple_of(i * group, group)
        factors = totals[pl.ds(slot0, group), :]
        mixing = [
            weights[pl.ds(at + g * tokens, tokens), :] * factors[g : g + 1, :]
            for g in range(group)
        ]
        mixing = jnp.concatenate(mixing, axis=0).astype(BF16)
        return total + lax.dot_general(
            mixing,
            docs[pl.ds(at, group * tokens), :],
            (((0,), (0,)), ((), ())),
            preferred_element_type=F32,
        )

    grad_q = lax.fori_loop(0, slots // group, add, jnp.zeros((queries_n, features), F32))
    along = jnp.sum(embedded * grad_q, axis=1, keepdims=True)
    grad_embedded = (inverse * grad_q - inverse * inverse * inverse * embedded * along).astype(BF16)
    packet[0:queries_n, :] = grad_embedded

    block = 8
    for i in range(head.shape[0] // (block * features)):
        sums = []
        for k in range(i * block, (i + 1) * block):
            at = slice(k * features, (k + 1) * features)
            grad_normed = lax.dot_general(
                grad_embedded, head[at, :], (((1,), (1,)), ((), ())), preferred_element_type=F32
            )
            sums.append(jnp.sum(grad_normed * unit[:, at], axis=0, keepdims=True))
        line = queries_n + i * block
        packet[line : line + block, :] = jnp.concatenate(sums, axis=0).astype(BF16)


def score(docs, embedded, spans, flags, unit, head):
    slots = flags.shape[0]
    queries_n, features = embedded.shape
    count = docs.shape[0]
    return pl.pallas_call(
        score_kernel,
        in_specs=[VMEM] * 6,
        out_specs=[VMEM] * 2,
        out_shape=[
            jax.ShapeDtypeStruct((slots, 1), F32),
            jax.ShapeDtypeStruct((queries_n + head.shape[0] // features, features), BF16),
        ],
        scratch_shapes=[
            pltpu.VMEM((count, queries_n), F32),
            pltpu.VMEM((slots, queries_n), F32),
        ],
        compiler_params=pltpu.CompilerParams(vmem_limit_bytes=32 * 1024 * 1024),
        cost_estimate=pl.CostEstimate(
            flops=4 * count * queries_n * features,
            bytes_accessed=30_000_000,
            transcendentals=count * queries_n,
        ),
        name="score",
    )(docs, embedded, spans, flags, unit, head)


def bundle_kernel(packets, unit, out, ge):
    count, tall, features = packets.shape
    tokens = unit.shape[0] // count
    shares, _, _ = out.shape
    total = jnp.zeros((tall - tokens, features), F32)
    for i in range(count):
        ge[i * tokens : (i + 1) * tokens, :] = packets[i, 0:tokens, :]
        total = total + packets[i, tokens:tall, :].astype(F32)
    head = lax.dot_general(
        ge[...], unit[...], (((0,), (0,)), ((), ())), preferred_element_type=F32
    ).T
    share = head.shape[0] // shares
    lines = total.shape[0] // shares
    for i in range(shares):
        out[i, 0:share, :] = head[i * share : (i + 1) * share].astype(BF16)
        gain = jnp.concatenate(
            [total[i * lines : (i + 1) * lines], jnp.zeros((16 - lines, features), F32)]
        )
        out[i, share : share + 16, :] = gain.astype(BF16)


def bundle(packets, unit, shares):
    count, tall, features = packets.shape
    return pl.pallas_call(
        bundle_kernel,
        in_specs=[VMEM] * 2,
        out_specs=VMEM,
        out_shape=jax.ShapeDtypeStruct((shares, unit.shape[1] // shares + 16, features), BF16),
        scratch_shapes=[pltpu.VMEM((unit.shape[0], features), BF16)],
        compiler_params=pltpu.CompilerParams(vmem_limit_bytes=32 * 1024 * 1024),
        name="bundle",
    )(packets, unit)


def local(
    residual,
    context,
    out_proj,
    norm_gain,
    colbert_head,
    candidates,
    lengths,
    centroid_ids,
    residual_codes,
    centroids,
    buckets,
):
    shards = Y * Z
    seq_rows, width = residual.shape
    cand_count = candidates.shape[1]
    per_shard, doc_len = centroid_ids.shape
    feature_dim = centroids.shape[1]
    cap = 2
    slots = shards * cap

    slot_ids = candidates.reshape(-1)
    owners = slot_ids // per_shard
    local_ids = slot_ids - owners * per_shard
    order = jnp.arange(cand_count, dtype=I32)
    earlier = (owners[None, :] == owners[:, None]) & (order[None, :] < order[:, None])
    rank = jnp.sum(earlier.astype(I32), axis=1)
    position = owners * cap + rank
    slot_at = jnp.arange(slots, dtype=I32)
    placed = position[None, :] == slot_at[:, None]
    request = jnp.sum(jnp.where(placed, local_ids[None, :], 0), axis=1)
    filled = jnp.any(placed, axis=1)
    flags = jnp.stack([filled, slot_at == position[0]], axis=1).astype(I32)
    note = jnp.concatenate(
        [
            jnp.broadcast_to(lengths[None, :], (shards, per_shard)),
            request.reshape(shards, cap),
            jnp.zeros((shards, 128 - per_shard - cap), I32),
        ],
        axis=1,
    )

    proj_z = lax.all_gather(out_proj, "z", axis=1, tiled=True)
    documents = decode_all(centroid_ids, residual_codes, centroids, buckets)
    notes = lax.all_to_all(note, DP, 0, 0, tiled=True)
    documents = documents.reshape(per_shard, doc_len, feature_dim)
    chosen = rows_of(documents, notes[:, per_shard : per_shard + cap].reshape(slots))
    chosen, colbert_head = lax.optimization_barrier((chosen, colbert_head))
    proj_z, context = lax.optimization_barrier((proj_z, context))
    got_docs = lax.all_to_all(
        chosen.reshape(shards, cap * doc_len, feature_dim), DP, 0, 0, tiled=True
    ).reshape(slots * doc_len, feature_dim)
    spans = jnp.sum(
        jnp.where(
            jnp.arange(per_shard, dtype=I32)[None, None, :]
            == request.reshape(shards, cap)[:, :, None],
            notes[:, None, :per_shard],
            0,
        ),
        axis=2,
    ).reshape(slots, 1)
    spans = jnp.broadcast_to(spans, (slots, seq_rows))

    here_x, here_c, here_y = lax.axis_index("x"), lax.axis_index("c"), lax.axis_index("y")
    blocks = context.reshape(X, C, seq_rows, context.shape[1])
    blocks = jnp.where(here_c == 0, blocks, blocks[:, ::-1])
    blocks = unxor(blocks, here_x).transpose(1, 0, 2, 3)
    by_y = jnp.stack([blocks] + [swap(blocks, "y", Y, step) for step in range(1, Y)], axis=2)
    by_y = by_y.reshape(C, X * Y * seq_rows, context.shape[1])

    head_pair = swap(colbert_head, "c", C, 1)
    head_pair = jnp.where(
        here_c == 0,
        jnp.stack([colbert_head, head_pair]),
        jnp.stack([head_pair, colbert_head]),
    )
    head_full = unxor(
        jnp.stack([head_pair] + [swap(head_pair, "x", X, step) for step in range(1, X)]), here_x
    ).reshape(width, feature_dim)
    head_rows = colbert_head.shape[0]
    mine = (here_x * C + here_c) * head_rows
    gain_blk = lax.dynamic_slice_in_dim(norm_gain, mine, head_rows, 0)
    by_y, head_full, proj_z, gain_blk = lax.optimization_barrier(
        (by_y, head_full, proj_z, gain_blk)
    )

    away = jnp.dot(by_y[1], proj_z, preferred_element_type=F32).astype(BF16)
    away = swap(away, "c", C, 1)
    stay = jnp.dot(by_y[0], proj_z, preferred_element_type=F32).astype(BF16)
    stay = lax.optimization_barrier(stay)
    pair = (stay.astype(F32) + away.astype(F32)).reshape(X, Y, seq_rows, width // Y)
    pieces, row = [pair[step].astype(BF16) for step in range(1, X)], pair[0]
    for step in range(1, X):
        row = row + swap(pieces[step - 1], "x", X, step).astype(F32)
    for_y = row.astype(BF16)
    columns = [for_y[0]] + [swap(for_y[step], "y", Y, step) for step in range(1, Y)]
    columns = unxor(jnp.stack(columns), here_y)
    attended = columns.transpose(1, 0, 2).reshape(seq_rows, width).astype(F32)
    summed = residual.astype(F32) + attended
    inv_rms = lax.rsqrt(jnp.mean(summed * summed, axis=-1, keepdims=True) + EPS)
    scaled_sum = summed * inv_rms
    normed = (scaled_sum * norm_gain).astype(BF16)
    embedded = jnp.dot(normed, head_full, preferred_element_type=F32)

    unit = scaled_sum.astype(BF16).reshape(seq_rows, X * C, head_rows).transpose(1, 0, 2)
    unit, got_docs = lax.optimization_barrier((unit, got_docs))
    unit_plane = lax.all_to_all(
        jnp.broadcast_to(unit, (Y,) + unit.shape).reshape((-1,) + unit.shape[1:]),
        PLANE,
        0,
        0,
        tiled=True,
    ).reshape(Y * X * C * seq_rows, head_rows)

    slot_scores, packet = score(got_docs, embedded, spans, flags, scaled_sum, head_full)
    packet, unit_plane = lax.optimization_barrier((packet, unit_plane))
    packets = lax.all_to_all(
        jnp.broadcast_to(packet, (Y * X * C,) + packet.shape), PLANE, 0, 0, tiled=True
    )
    ge_plane = packets[:, :seq_rows]

    proj_full = lax.all_gather(proj_z, "y", axis=1, tiled=True)
    packets, summed_all, proj_full = lax.optimization_barrier(
        (packets, summed.astype(BF16), proj_full)
    )
    summed_all = lax.all_gather(summed_all, TENSOR, axis=0, tiled=True)

    share = head_rows // Z
    lines = width // feature_dim // Z
    first = bundle(packets, unit_plane, Z)
    first, slot_scores, ge_plane = lax.optimization_barrier((first, slot_scores, ge_plane))
    scores = jnp.sum(jnp.where(placed, slot_scores, 0.0), axis=0)[None, :]
    first = lax.all_to_all(first, "z", 0, 0, tiled=True)
    second = jnp.sum(first.astype(F32), axis=0, keepdims=True).astype(BF16)
    packet, packets = lax.optimization_barrier((packet, packets))
    grad_embedded = packet[:seq_rows]
    grad_normed = lax.dot_general(
        grad_embedded, head_full, (((1,), (1,)), ((), ())), preferred_element_type=F32
    )
    scaled = grad_normed * norm_gain
    residual_grad = (
        inv_rms * scaled - summed * inv_rms**3 * jnp.mean(summed * scaled, axis=-1, keepdims=True)
    ).astype(BF16)
    ge_all = lax.dynamic_slice_in_dim(ge_plane, here_y * (X * C), X * C, 0)
    ge_all = ge_all.reshape(X * C * seq_rows, feature_dim)
    gained_head = (head_full.astype(F32) * norm_gain[:, None]).astype(BF16)
    mixed_head = jnp.dot(proj_full, gained_head, preferred_element_type=F32).astype(BF16)
    second, mixed_head, residual_grad = lax.optimization_barrier(
        (second, mixed_head, residual_grad)
    )
    second = lax.all_to_all(
        jnp.broadcast_to(second, (Z,) + second.shape[1:]), "z", 0, 0, tiled=True
    )
    pulled = lax.dot_general(
        summed_all, proj_full, (((1,), (1,)), ((), ())), preferred_element_type=F32
    )
    wide = summed_all.astype(F32)
    inv_all = lax.rsqrt(jnp.mean(wide * wide, axis=-1, keepdims=True) + EPS)
    embedded_all = jnp.dot(summed_all, gained_head, preferred_element_type=F32)
    pull_all = jnp.sum(ge_all.astype(F32) * embedded_all, axis=-1, keepdims=True) * (1.0 / width)
    context_grad = (
        inv_all
        * lax.dot_general(
            ge_all, mixed_head, (((1,), (1,)), ((), ())), preferred_element_type=F32
        )
        - inv_all**3 * pull_all * pulled
    ).astype(BF16)

    second, context_grad = lax.optimization_barrier((second, context_grad))
    head_grad = second[:, :share].astype(F32).reshape(head_rows, feature_dim) * gain_blk[:, None]
    gain_grad = second[:, share : share + lines].astype(F32).reshape(width)
    return (scores, context_grad, residual_grad, head_grad, gain_grad)


def solution(mesh):
    split = Mesh(mesh.devices.reshape(Y, Z, X, C), ("y", "z", "x", "c"))
    both = DP + TENSOR
    in_specs = (
        P(both, None),
        P(DP, TENSOR),
        P(TENSOR, DP),
        P(),
        P(TENSOR, None),
        P(both, None),
        P(DP),
        P(DP, None),
        P(DP, None),
        P(),
        P(),
    )
    out_specs = (
        P(both, None),
        P(DP, TENSOR),
        P(both, None),
        P(TENSOR, None),
        P(),
    )
    return jax.shard_map(local, mesh=split, in_specs=in_specs, out_specs=out_specs, check_vma=False)
```

```python
import jax
import jax.numpy as jnp
from jax import lax
from jax.experimental import pallas as pl
from jax.experimental.pallas import tpu as pltpu
from jax.sharding import Mesh, PartitionSpec as P

EPS = 1e-06
TEMPER = 0.1
LOSS_SCALE = 64.0

Y, Z, X, C = 4, 16, 4, 2
DP = ("y", "z")
TENSOR = ("x", "c")
PLANE = ("y", "x", "c")

BF16 = jnp.bfloat16
F32 = jnp.float32
I32 = jnp.int32
VMEM = pl.BlockSpec(memory_space=pltpu.VMEM)
SMEM = pl.BlockSpec(memory_space=pltpu.SMEM)


def swap(values, axis, size, step):
    return lax.ppermute(values, axis, [(i, i ^ step) for i in range(size)])


def rows_of(values, index):
    return values.at[index].get(mode="promise_in_bounds")


def unxor(blocks, place):
    return rows_of(blocks, jnp.arange(blocks.shape[0], dtype=I32) ^ place)


def decode_kernel(buckets, packed, rows, out):
    words = packed.shape[1]
    features = out.shape[1]
    feature = lax.broadcasted_iota(I32, (words, features), 1)
    word = lax.broadcasted_iota(I32, (words, features), 0)
    here = (feature >> 3) == word
    first = (feature & 7) < 4
    spread_low = jnp.where(here & first, 1.0, 0.0).astype(BF16)
    spread_high = jnp.where(here & ~first, 1.0, 0.0).astype(BF16)
    step = 256
    shift = 2 * (lax.broadcasted_iota(I32, (step, features), 1) & 3)
    zero, one, two, three = [buckets[k] for k in range(4)]

    @pl.loop(0, out.shape[0] // step)
    def _(i):
        at = pl.ds(pl.multiple_of(i * step, step), step)
        codes = packed[at, :]
        code_bytes = jnp.dot(
            (codes & 255).astype(F32).astype(BF16), spread_low, preferred_element_type=F32
        ) + jnp.dot(
            ((codes >> 8) & 255).astype(F32).astype(BF16), spread_high, preferred_element_type=F32
        )
        codes = (code_bytes.astype(I32) >> shift) & 3
        low = (codes & 1).astype(F32)
        high = (codes >> 1).astype(F32)
        levels = zero + low * (one - zero) + high * (two - zero)
        levels = levels + low * high * (three - two - one + zero)
        vectors = rows[at, :].astype(F32) + levels
        scale = lax.rsqrt(jnp.sum(vectors * vectors, axis=1, keepdims=True) + EPS)
        out[at, :] = (vectors * scale).astype(BF16)


def decode_all(cell_ids, packed, centroids, buckets):
    count = cell_ids.size
    packed = packed.reshape(count, packed.size // count)
    rows = rows_of(centroids, cell_ids.reshape(count))
    return pl.pallas_call(
        decode_kernel,
        in_specs=[SMEM, VMEM, VMEM],
        out_specs=VMEM,
        out_shape=jax.ShapeDtypeStruct((count, centroids.shape[1]), BF16),
        compiler_params=pltpu.CompilerParams(vmem_limit_bytes=32 * 1024 * 1024),
        name="decode",
    )(buckets, packed, rows)


def score_kernel(docs, embedded_ref, spans, flags, unit, head, scores, packet, weights, totals):
    slots, queries_n = totals.shape
    tokens = docs.shape[0] // slots
    features = docs.shape[1]
    embedded = embedded_ref[...]
    inverse = lax.rsqrt(jnp.sum(embedded * embedded, axis=1, keepdims=True) + EPS)
    queries = (embedded * inverse).astype(BF16)
    group = 8
    token = lax.broadcasted_iota(I32, (tokens, queries_n), 0)

    @pl.loop(0, slots // group)
    def _(i):
        at = pl.multiple_of(i * (group * tokens), group * tokens)
        slot0 = pl.multiple_of(i * group, group)
        similar = lax.dot_general(
            docs[pl.ds(at, group * tokens), :],
            queries,
            (((1,), (1,)), ((), ())),
            preferred_element_type=F32,
        )
        sizes = spans[pl.ds(slot0, group), :]
        sums = []
        for g in range(group):
            one = jnp.exp(similar[g * tokens : (g + 1) * tokens] / TEMPER)
            one = jnp.where(token < sizes[g : g + 1, :], one, 0.0)
            weights[pl.ds(at + g * tokens, tokens), :] = one
            sums.append(jnp.sum(one, axis=0, keepdims=True))
        totals[pl.ds(slot0, group), :] = jnp.concatenate(sums, axis=0)

    all_totals = totals[...]
    slot_scores = TEMPER * jnp.sum(jnp.log(all_totals), axis=1, keepdims=True)
    scores[...] = slot_scores
    filled = flags[:, 0:1] > 0
    positive = flags[:, 1:2] > 0
    exponent = jnp.where(filled, jnp.exp(slot_scores), 0.0)
    share = exponent / jnp.sum(exponent, axis=0, keepdims=True)
    seeds = LOSS_SCALE * (share - jnp.where(positive, 1.0, 0.0))
    totals[...] = seeds / all_totals

    def add(i, total):
        at = pl.multiple_of(i * (group * tokens), group * tokens)
        slot0 = pl.multiple_of(i * group, group)
        factors = totals[pl.ds(slot0, group), :]
        mixing = [
            weights[pl.ds(at + g * tokens, tokens), :] * factors[g : g + 1, :]
            for g in range(group)
        ]
        mixing = jnp.concatenate(mixing, axis=0).astype(BF16)
        return total + lax.dot_general(
            mixing,
            docs[pl.ds(at, group * tokens), :],
            (((0,), (0,)), ((), ())),
            preferred_element_type=F32,
        )

    grad_q = lax.fori_loop(0, slots // group, add, jnp.zeros((queries_n, features), F32))
    along = jnp.sum(embedded * grad_q, axis=1, keepdims=True)
    grad_embedded = (inverse * grad_q - inverse * inverse * inverse * embedded * along).astype(BF16)
    packet[0:queries_n, :] = grad_embedded

    block = 8
    for i in range(head.shape[0] // (block * features)):
        sums = []
        for k in range(i * block, (i + 1) * block):
            at = slice(k * features, (k + 1) * features)
            grad_normed = lax.dot_general(
                grad_embedded, head[at, :], (((1,), (1,)), ((), ())), preferred_element_type=F32
            )
            sums.append(jnp.sum(grad_normed * unit[:, at], axis=0, keepdims=True))
        line = queries_n + i * block
        packet[line : line + block, :] = jnp.concatenate(sums, axis=0).astype(BF16)


def score(docs, embedded, spans, flags, unit, head):
    slots = flags.shape[0]
    queries_n, features = embedded.shape
    count = docs.shape[0]
    return pl.pallas_call(
        score_kernel,
        in_specs=[VMEM] * 6,
        out_specs=[VMEM] * 2,
        out_shape=[
            jax.ShapeDtypeStruct((slots, 1), F32),
            jax.ShapeDtypeStruct((queries_n + head.shape[0] // features, features), BF16),
        ],
        scratch_shapes=[
            pltpu.VMEM((count, queries_n), F32),
            pltpu.VMEM((slots, queries_n), F32),
        ],
        compiler_params=pltpu.CompilerParams(vmem_limit_bytes=32 * 1024 * 1024),
        cost_estimate=pl.CostEstimate(
            flops=4 * count * queries_n * features,
            bytes_accessed=30_000_000,
            transcendentals=count * queries_n,
        ),
        name="score",
    )(docs, embedded, spans, flags, unit, head)


def bundle_kernel(here, packets, *refs):
    *units, out, ge = refs
    count, tall, features = packets.shape
    rows = units[0].shape[0]
    tokens = len(units) * rows // count
    shares, _, _ = out.shape
    total = jnp.zeros((tall - tokens, features), F32)
    for i in range(count):
        ge[i * tokens : (i + 1) * tokens, :] = packets[here[0] ^ i, 0:tokens, :]
        total = total + packets[i, tokens:tall, :].astype(F32)
    head = jnp.zeros((features, units[0].shape[1]), F32)
    for i, unit in enumerate(units):
        head = head + lax.dot_general(
            ge[i * rows : (i + 1) * rows, :],
            unit[...],
            (((0,), (0,)), ((), ())),
            preferred_element_type=F32,
        )
    head = head.T
    share = head.shape[0] // shares
    lines = total.shape[0] // shares
    for i in range(shares):
        out[i, 0:share, :] = head[i * share : (i + 1) * share].astype(BF16)
        gain = jnp.concatenate(
            [total[i * lines : (i + 1) * lines], jnp.zeros((16 - lines, features), F32)]
        )
        out[i, share : share + 16, :] = gain.astype(BF16)


def bundle(here, packets, units, shares):
    count, tall, features = packets.shape
    return pl.pallas_call(
        bundle_kernel,
        in_specs=[SMEM] + [VMEM] * (1 + len(units)),
        out_specs=VMEM,
        out_shape=jax.ShapeDtypeStruct((shares, units[0].shape[1] // shares + 16, features), BF16),
        scratch_shapes=[pltpu.VMEM((len(units) * units[0].shape[0], features), BF16)],
        compiler_params=pltpu.CompilerParams(vmem_limit_bytes=32 * 1024 * 1024),
        name="bundle",
    )(here, packets, *units)


def local(
    residual,
    context,
    out_proj,
    norm_gain,
    colbert_head,
    candidates,
    lengths,
    centroid_ids,
    residual_codes,
    centroids,
    buckets,
):
    shards = Y * Z
    seq_rows, width = residual.shape
    cand_count = candidates.shape[1]
    per_shard, doc_len = centroid_ids.shape
    feature_dim = centroids.shape[1]
    cap = 2
    slots = shards * cap

    slot_ids = candidates.reshape(-1)
    owners = slot_ids // per_shard
    local_ids = slot_ids - owners * per_shard
    order = jnp.arange(cand_count, dtype=I32)
    earlier = (owners[None, :] == owners[:, None]) & (order[None, :] < order[:, None])
    rank = jnp.sum(earlier.astype(I32), axis=1)
    position = owners * cap + rank
    slot_at = jnp.arange(slots, dtype=I32)
    placed = position[None, :] == slot_at[:, None]
    request = jnp.sum(jnp.where(placed, local_ids[None, :], 0), axis=1)
    filled = jnp.any(placed, axis=1)
    flags = jnp.stack([filled, slot_at == position[0]], axis=1).astype(I32)
    note = jnp.concatenate(
        [
            jnp.broadcast_to(lengths[None, :], (shards, per_shard)),
            request.reshape(shards, cap),
            jnp.zeros((shards, 128 - per_shard - cap), I32),
        ],
        axis=1,
    )

    proj_z = lax.all_gather(out_proj, "z", axis=1, tiled=True)
    documents = decode_all(centroid_ids, residual_codes, centroids, buckets)
    notes = lax.all_to_all(note, DP, 0, 0, tiled=True)
    documents = documents.reshape(per_shard, doc_len, feature_dim)
    chosen = rows_of(documents, notes[:, per_shard : per_shard + cap].reshape(slots))
    chosen, context = lax.optimization_barrier((chosen, context))
    got_docs = lax.all_to_all(
        chosen.reshape(shards, cap * doc_len, feature_dim), DP, 0, 0, tiled=True
    ).reshape(slots * doc_len, feature_dim)
    spans = jnp.sum(
        jnp.where(
            jnp.arange(per_shard, dtype=I32)[None, None, :]
            == request.reshape(shards, cap)[:, :, None],
            notes[:, None, :per_shard],
            0,
        ),
        axis=2,
    ).reshape(slots, 1)
    spans = jnp.broadcast_to(spans, (slots, seq_rows))

    here_x, here_c, here_y = lax.axis_index("x"), lax.axis_index("c"), lax.axis_index("y")
    blocks = context.reshape(X, C, seq_rows, context.shape[1])
    blocks = jnp.where(here_c == 0, blocks, blocks[:, ::-1])
    blocks = unxor(blocks, here_x).transpose(1, 0, 2, 3)
    by_y = jnp.stack([blocks] + [swap(blocks, "y", Y, step) for step in range(1, Y)], axis=2)
    by_y = by_y.reshape(C, X * Y * seq_rows, context.shape[1])

    head_rows = colbert_head.shape[0]
    mine = (here_x * C + here_c) * head_rows
    gain_blk = lax.dynamic_slice_in_dim(norm_gain, mine, head_rows, 0)
    by_y, proj_z, gain_blk, colbert_head = lax.optimization_barrier(
        (by_y, proj_z, gain_blk, colbert_head)
    )
    head_full = lax.all_gather(colbert_head, TENSOR, axis=0, tiled=True)

    away = jnp.dot(by_y[1], proj_z, preferred_element_type=F32).astype(BF16)
    away = swap(away, "c", C, 1)
    stay = jnp.dot(by_y[0], proj_z, preferred_element_type=F32).astype(BF16)
    stay = lax.optimization_barrier(stay)
    pair = (stay.astype(F32) + away.astype(F32)).reshape(X, Y, seq_rows, width // Y)
    pieces, row = [pair[step].astype(BF16) for step in range(1, X)], pair[0]
    for step in range(1, X):
        row = row + swap(pieces[step - 1], "x", X, step).astype(F32)
    for_y = row.astype(BF16)
    columns = [for_y[0]] + [swap(for_y[step], "y", Y, step) for step in range(1, Y)]
    columns = unxor(jnp.stack(columns), here_y)
    attended = columns.transpose(1, 0, 2).reshape(seq_rows, width).astype(F32)
    summed = residual.astype(F32) + attended
    inv_rms = lax.rsqrt(jnp.mean(summed * summed, axis=-1, keepdims=True) + EPS)
    scaled_sum = summed * inv_rms
    normed = (scaled_sum * norm_gain).astype(BF16)

    unit = scaled_sum.astype(BF16).reshape(seq_rows, X, C, head_rows).transpose(1, 2, 0, 3)
    unit = unxor(jnp.where(here_c == 0, unit, unit[:, ::-1]), here_x)
    unit = jnp.stack([unit[:, 0], swap(unit[:, 1], "c", C, 1)], axis=1)
    unit = jnp.stack([unit[0]] + [swap(unit[step], "x", X, step) for step in range(1, X)])
    unit, normed, got_docs = lax.optimization_barrier((unit, normed, got_docs))
    unit = unit.reshape(X * C * seq_rows, head_rows)
    units = [unit] + [swap(unit, "y", Y, step) for step in range(1, Y)]

    embedded = jnp.dot(normed, head_full, preferred_element_type=F32)
    slot_scores, packet = score(got_docs, embedded, spans, flags, scaled_sum, head_full)
    packets = lax.all_to_all(
        jnp.broadcast_to(packet, (Y * X * C,) + packet.shape), PLANE, 0, 0, tiled=True
    )
    ge_plane = packets[:, :seq_rows]


    share = head_rows // Z
    lines = width // feature_dim // Z
    here = ((here_y * X + here_x) * C + here_c).reshape(1)
    first = bundle(here, packets, units, Z)
    first, slot_scores, ge_plane = lax.optimization_barrier((first, slot_scores, ge_plane))
    scores = jnp.sum(jnp.where(placed, slot_scores, 0.0), axis=0)[None, :]
    proj_full = lax.all_gather(proj_z, "y", axis=1, tiled=True)
    marker, summed_all, proj_full = lax.optimization_barrier(
        (first, summed.astype(BF16), proj_full)
    )
    summed_all = lax.all_gather(summed_all, TENSOR, axis=0, tiled=True)
    first = lax.all_to_all(first, "z", 0, 0, tiled=True)
    second = jnp.sum(first.astype(F32), axis=0, keepdims=True).astype(BF16)
    packet, packets = lax.optimization_barrier((packet, packets))
    grad_embedded = packet[:seq_rows]
    grad_normed = lax.dot_general(
        grad_embedded, head_full, (((1,), (1,)), ((), ())), preferred_element_type=F32
    )
    scaled = grad_normed * norm_gain
    residual_grad = (
        inv_rms * scaled - summed * inv_rms**3 * jnp.mean(summed * scaled, axis=-1, keepdims=True)
    ).astype(BF16)
    ge_all = lax.dynamic_slice_in_dim(ge_plane, here_y * (X * C), X * C, 0)
    ge_all = ge_all.reshape(X * C * seq_rows, feature_dim)
    gained_head = (head_full.astype(F32) * norm_gain[:, None]).astype(BF16)
    mixed_head = jnp.dot(proj_full, gained_head, preferred_element_type=F32).astype(BF16)
    second, mixed_head, residual_grad = lax.optimization_barrier(
        (second, mixed_head, residual_grad)
    )
    second = lax.all_to_all(
        jnp.broadcast_to(second, (Z,) + second.shape[1:]), "z", 0, 0, tiled=True
    )
    pulled = lax.dot_general(
        summed_all, proj_full, (((1,), (1,)), ((), ())), preferred_element_type=F32
    )
    wide = summed_all.astype(F32)
    inv_all = lax.rsqrt(jnp.mean(wide * wide, axis=-1, keepdims=True) + EPS)
    embedded_all = jnp.dot(summed_all, gained_head, preferred_element_type=F32)
    pull_all = jnp.sum(ge_all.astype(F32) * embedded_all, axis=-1, keepdims=True) * (1.0 / width)
    context_grad = (
        inv_all
        * lax.dot_general(
            ge_all, mixed_head, (((1,), (1,)), ((), ())), preferred_element_type=F32
        )
        - inv_all**3 * pull_all * pulled
    ).astype(BF16)

    second, context_grad = lax.optimization_barrier((second, context_grad))
    head_grad = second[:, :share].astype(F32).reshape(head_rows, feature_dim) * gain_blk[:, None]
    gain_grad = second[:, share : share + lines].astype(F32).reshape(width)
    return (scores, context_grad, residual_grad, head_grad, gain_grad)


def solution(mesh):
    split = Mesh(mesh.devices.reshape(Y, Z, X, C), ("y", "z", "x", "c"))
    both = DP + TENSOR
    in_specs = (
        P(both, None),
        P(DP, TENSOR),
        P(TENSOR, DP),
        P(),
        P(TENSOR, None),
        P(both, None),
        P(DP),
        P(DP, None),
        P(DP, None),
        P(),
        P(),
    )
    out_specs = (
        P(both, None),
        P(DP, TENSOR),
        P(both, None),
        P(TENSOR, None),
        P(),
    )
    return jax.shard_map(local, mesh=split, in_specs=in_specs, out_specs=out_specs, check_vma=False)
```

```python
import jax
import jax.numpy as jnp
from jax import lax
from jax.experimental import pallas as pl
from jax.experimental.pallas import tpu as pltpu
from jax.sharding import Mesh, PartitionSpec as P

EPS = 1e-06
TEMPER = 0.1
LOSS_SCALE = 64.0

Y, Z, X, C = 4, 16, 4, 2
DP = ("y", "z")
TENSOR = ("x", "c")
PLANE = ("y", "x", "c")

BF16 = jnp.bfloat16
F32 = jnp.float32
I32 = jnp.int32
VMEM = pl.BlockSpec(memory_space=pltpu.VMEM)
SMEM = pl.BlockSpec(memory_space=pltpu.SMEM)


def swap(values, axis, size, step):
    return lax.ppermute(values, axis, [(i, i ^ step) for i in range(size)])


def rows_of(values, index):
    return values.at[index].get(mode="promise_in_bounds")


def unxor(blocks, place):
    return rows_of(blocks, jnp.arange(blocks.shape[0], dtype=I32) ^ place)


def decode_kernel(buckets, packed, rows, out):
    words = packed.shape[1]
    features = out.shape[1]
    feature = lax.broadcasted_iota(I32, (words, features), 1)
    word = lax.broadcasted_iota(I32, (words, features), 0)
    here = (feature >> 3) == word
    first = (feature & 7) < 4
    spread_low = jnp.where(here & first, 1.0, 0.0).astype(BF16)
    spread_high = jnp.where(here & ~first, 1.0, 0.0).astype(BF16)
    step = 256
    shift = 2 * (lax.broadcasted_iota(I32, (step, features), 1) & 3)
    zero, one, two, three = [buckets[k] for k in range(4)]

    @pl.loop(0, out.shape[0] // step)
    def _(i):
        at = pl.ds(pl.multiple_of(i * step, step), step)
        codes = packed[at, :]
        code_bytes = jnp.dot(
            (codes & 255).astype(F32).astype(BF16), spread_low, preferred_element_type=F32
        ) + jnp.dot(
            ((codes >> 8) & 255).astype(F32).astype(BF16), spread_high, preferred_element_type=F32
        )
        codes = (code_bytes.astype(I32) >> shift) & 3
        low = (codes & 1).astype(F32)
        high = (codes >> 1).astype(F32)
        levels = zero + low * (one - zero) + high * (two - zero)
        levels = levels + low * high * (three - two - one + zero)
        vectors = rows[at, :].astype(F32) + levels
        scale = lax.rsqrt(jnp.sum(vectors * vectors, axis=1, keepdims=True) + EPS)
        out[at, :] = (vectors * scale).astype(BF16)


def decode_all(cell_ids, packed, centroids, buckets):
    count = cell_ids.size
    packed = packed.reshape(count, packed.size // count)
    rows = rows_of(centroids, cell_ids.reshape(count))
    return pl.pallas_call(
        decode_kernel,
        in_specs=[SMEM, VMEM, VMEM],
        out_specs=VMEM,
        out_shape=jax.ShapeDtypeStruct((count, centroids.shape[1]), BF16),
        compiler_params=pltpu.CompilerParams(vmem_limit_bytes=32 * 1024 * 1024),
        name="decode",
    )(buckets, packed, rows)


def score_kernel(docs, embedded_ref, spans, flags, unit, head, scores, packets, weights, totals):
    slots, queries_n = totals.shape
    tokens = docs.shape[0] // slots
    features = docs.shape[1]
    embedded = embedded_ref[...]
    inverse = lax.rsqrt(jnp.sum(embedded * embedded, axis=1, keepdims=True) + EPS)
    queries = (embedded * inverse).astype(BF16)
    group = 8
    token = lax.broadcasted_iota(I32, (tokens, queries_n), 0)

    @pl.loop(0, slots // group)
    def _(i):
        at = pl.multiple_of(i * (group * tokens), group * tokens)
        slot0 = pl.multiple_of(i * group, group)
        similar = lax.dot_general(
            docs[pl.ds(at, group * tokens), :],
            queries,
            (((1,), (1,)), ((), ())),
            preferred_element_type=F32,
        )
        sizes = spans[pl.ds(slot0, group), :]
        sums = []
        for g in range(group):
            one = jnp.exp(similar[g * tokens : (g + 1) * tokens] / TEMPER)
            one = jnp.where(token < sizes[g : g + 1, :], one, 0.0)
            weights[pl.ds(at + g * tokens, tokens), :] = one
            sums.append(jnp.sum(one, axis=0, keepdims=True))
        totals[pl.ds(slot0, group), :] = jnp.concatenate(sums, axis=0)

    all_totals = totals[...]
    slot_scores = TEMPER * jnp.sum(jnp.log(all_totals), axis=1, keepdims=True)
    scores[...] = slot_scores
    filled = flags[:, 0:1] > 0
    positive = flags[:, 1:2] > 0
    exponent = jnp.where(filled, jnp.exp(slot_scores), 0.0)
    share = exponent / jnp.sum(exponent, axis=0, keepdims=True)
    seeds = LOSS_SCALE * (share - jnp.where(positive, 1.0, 0.0))
    totals[...] = seeds / all_totals

    def add(i, total):
        at = pl.multiple_of(i * (group * tokens), group * tokens)
        slot0 = pl.multiple_of(i * group, group)
        factors = totals[pl.ds(slot0, group), :]
        mixing = [
            weights[pl.ds(at + g * tokens, tokens), :] * factors[g : g + 1, :]
            for g in range(group)
        ]
        mixing = jnp.concatenate(mixing, axis=0).astype(BF16)
        return total + lax.dot_general(
            mixing,
            docs[pl.ds(at, group * tokens), :],
            (((0,), (0,)), ((), ())),
            preferred_element_type=F32,
        )

    grad_q = lax.fori_loop(0, slots // group, add, jnp.zeros((queries_n, features), F32))
    along = jnp.sum(embedded * grad_q, axis=1, keepdims=True)
    grad_embedded = (inverse * grad_q - inverse * inverse * inverse * embedded * along).astype(BF16)
    copies = packets.shape[0]
    for k in range(copies):
        packets[k, 0:queries_n, :] = grad_embedded

    block = 8
    lines = []
    for i in range(head.shape[0] // (block * features)):
        sums = []
        for k in range(i * block, (i + 1) * block):
            at = slice(k * features, (k + 1) * features)
            grad_normed = lax.dot_general(
                grad_embedded, head[at, :], (((1,), (1,)), ((), ())), preferred_element_type=F32
            )
            sums.append(jnp.sum(grad_normed * unit[:, at], axis=0, keepdims=True))
        lines.append(jnp.concatenate(sums, axis=0))
    gain = jnp.concatenate(lines, axis=0).astype(BF16)
    base = queries_n + gain.shape[0]
    for k in range(copies):
        packets[k, queries_n:base, :] = gain

    parts = (packets.shape[1] - base) // queries_n
    sets = head.shape[0] // (parts * features)
    for j in range(sets):
        for part in range(parts):
            at = (j * parts + part) * features
            piece = unit[:, at : at + features].astype(BF16)
            row = base + part * queries_n
            for k in range(j, copies, sets):
                packets[k, row : row + queries_n, :] = piece


def score(docs, embedded, spans, flags, unit, head, copies, sets):
    slots = flags.shape[0]
    queries_n, features = embedded.shape
    count = docs.shape[0]
    lines = head.shape[0] // features
    tall = queries_n + lines + lines // sets * queries_n
    return pl.pallas_call(
        score_kernel,
        in_specs=[VMEM] * 6,
        out_specs=[VMEM] * 2,
        out_shape=[
            jax.ShapeDtypeStruct((slots, 1), F32),
            jax.ShapeDtypeStruct((copies, tall, features), BF16),
        ],
        scratch_shapes=[
            pltpu.VMEM((count, queries_n), F32),
            pltpu.VMEM((slots, queries_n), F32),
        ],
        compiler_params=pltpu.CompilerParams(vmem_limit_bytes=32 * 1024 * 1024),
        cost_estimate=pl.CostEstimate(
            flops=4 * count * queries_n * features,
            bytes_accessed=30_000_000,
            transcendentals=count * queries_n,
        ),
        name="score",
    )(docs, embedded, spans, flags, unit, head)


def bundle_kernel(packets, out, sides):
    count, _, features = packets.shape
    shares, tall, _ = out.shape
    share = tall - 16
    parts = sides.shape[0] - 1
    tokens = sides.shape[1] // count
    base = packets.shape[1] - parts * tokens
    total = jnp.zeros((base - tokens, features), F32)
    for i in range(count):
        sides[0, i * tokens : (i + 1) * tokens, :] = packets[i, 0:tokens, :]
        total = total + packets[i, tokens:base, :].astype(F32)
        for part in range(parts):
            row = base + part * tokens
            sides[part + 1, i * tokens : (i + 1) * tokens, :] = packets[i, row : row + tokens, :]
    lines = total.shape[0] // shares
    each = features // share
    for part in range(parts):
        head = lax.dot_general(
            sides[0], sides[part + 1], (((0,), (0,)), ((), ())), preferred_element_type=F32
        ).T
        for k in range(each):
            out[part * each + k, 0:share, :] = head[k * share : (k + 1) * share].astype(BF16)
    for i in range(shares):
        gain = jnp.concatenate(
            [total[i * lines : (i + 1) * lines], jnp.zeros((16 - lines, features), F32)]
        )
        out[i, share : share + 16, :] = gain.astype(BF16)


def bundle(packets, tokens, lines, shares):
    count, tall, features = packets.shape
    parts = (tall - tokens - lines) // tokens
    return pl.pallas_call(
        bundle_kernel,
        in_specs=[VMEM],
        out_specs=VMEM,
        out_shape=jax.ShapeDtypeStruct((shares, parts * features // shares + 16, features), BF16),
        scratch_shapes=[pltpu.VMEM((parts + 1, count * tokens, features), BF16)],
        compiler_params=pltpu.CompilerParams(vmem_limit_bytes=32 * 1024 * 1024),
        name="bundle",
    )(packets)


def local(
    residual,
    context,
    out_proj,
    norm_gain,
    colbert_head,
    candidates,
    lengths,
    centroid_ids,
    residual_codes,
    centroids,
    buckets,
):
    shards = Y * Z
    seq_rows, width = residual.shape
    cand_count = candidates.shape[1]
    per_shard, doc_len = centroid_ids.shape
    feature_dim = centroids.shape[1]
    cap = 2
    slots = shards * cap

    slot_ids = candidates.reshape(-1)
    owners = slot_ids // per_shard
    local_ids = slot_ids - owners * per_shard
    order = jnp.arange(cand_count, dtype=I32)
    earlier = (owners[None, :] == owners[:, None]) & (order[None, :] < order[:, None])
    rank = jnp.sum(earlier.astype(I32), axis=1)
    position = owners * cap + rank
    slot_at = jnp.arange(slots, dtype=I32)
    placed = position[None, :] == slot_at[:, None]
    request = jnp.sum(jnp.where(placed, local_ids[None, :], 0), axis=1)
    filled = jnp.any(placed, axis=1)
    flags = jnp.stack([filled, slot_at == position[0]], axis=1).astype(I32)
    note = jnp.concatenate(
        [
            jnp.broadcast_to(lengths[None, :], (shards, per_shard)),
            request.reshape(shards, cap),
            jnp.zeros((shards, 128 - per_shard - cap), I32),
        ],
        axis=1,
    )

    proj_z = lax.all_gather(out_proj, "z", axis=1, tiled=True)
    documents = decode_all(centroid_ids, residual_codes, centroids, buckets)
    notes = lax.all_to_all(note, DP, 0, 0, tiled=True)
    documents = documents.reshape(per_shard, doc_len, feature_dim)
    chosen = rows_of(documents, notes[:, per_shard : per_shard + cap].reshape(slots))
    chosen, colbert_head = lax.optimization_barrier((chosen, colbert_head))
    proj_z, context = lax.optimization_barrier((proj_z, context))
    got_docs = lax.all_to_all(
        chosen.reshape(shards, cap * doc_len, feature_dim), DP, 0, 0, tiled=True
    ).reshape(slots * doc_len, feature_dim)
    spans = jnp.sum(
        jnp.where(
            jnp.arange(per_shard, dtype=I32)[None, None, :]
            == request.reshape(shards, cap)[:, :, None],
            notes[:, None, :per_shard],
            0,
        ),
        axis=2,
    ).reshape(slots, 1)
    spans = jnp.broadcast_to(spans, (slots, seq_rows))

    here_x, here_c, here_y = lax.axis_index("x"), lax.axis_index("c"), lax.axis_index("y")
    blocks = context.reshape(X, C, seq_rows, context.shape[1])
    blocks = jnp.where(here_c == 0, blocks, blocks[:, ::-1])
    blocks = unxor(blocks, here_x).transpose(1, 0, 2, 3)
    by_y = jnp.stack([blocks] + [swap(blocks, "y", Y, step) for step in range(1, Y)], axis=2)
    by_y = by_y.reshape(C, X * Y * seq_rows, context.shape[1])

    head_pair = swap(colbert_head, "c", C, 1)
    head_pair = jnp.where(
        here_c == 0,
        jnp.stack([colbert_head, head_pair]),
        jnp.stack([head_pair, colbert_head]),
    )
    head_full = unxor(
        jnp.stack([head_pair] + [swap(head_pair, "x", X, step) for step in range(1, X)]), here_x
    ).reshape(width, feature_dim)
    head_rows = colbert_head.shape[0]
    mine = (here_x * C + here_c) * head_rows
    gain_blk = lax.dynamic_slice_in_dim(norm_gain, mine, head_rows, 0)
    by_y, head_full, proj_z, gain_blk = lax.optimization_barrier(
        (by_y, head_full, proj_z, gain_blk)
    )

    away = jnp.dot(by_y[1], proj_z, preferred_element_type=F32).astype(BF16)
    away = swap(away, "c", C, 1)
    stay = jnp.dot(by_y[0], proj_z, preferred_element_type=F32).astype(BF16)
    stay = lax.optimization_barrier(stay)
    pair = (stay.astype(F32) + away.astype(F32)).reshape(X, Y, seq_rows, width // Y)
    pieces, row = [pair[step].astype(BF16) for step in range(1, X)], pair[0]
    for step in range(1, X):
        row = row + swap(pieces[step - 1], "x", X, step).astype(F32)
    for_y = row.astype(BF16)
    columns = [for_y[0]] + [swap(for_y[step], "y", Y, step) for step in range(1, Y)]
    columns = unxor(jnp.stack(columns), here_y)
    attended = columns.transpose(1, 0, 2).reshape(seq_rows, width).astype(F32)
    summed = residual.astype(F32) + attended
    inv_rms = lax.rsqrt(jnp.mean(summed * summed, axis=-1, keepdims=True) + EPS)
    scaled_sum = summed * inv_rms
    normed = (scaled_sum * norm_gain).astype(BF16)
    embedded = jnp.dot(normed, head_full, preferred_element_type=F32)

    scaled_sum, got_docs = lax.optimization_barrier((scaled_sum, got_docs))
    slot_scores, packets = score(
        got_docs, embedded, spans, flags, scaled_sum, head_full, Y * X * C, X * C
    )
    grad_embedded = packets[0, :seq_rows]
    packets = lax.all_to_all(packets, PLANE, 0, 0, tiled=True)
    ge_plane = packets[:, :seq_rows]

    proj_full = lax.all_gather(proj_z, "y", axis=1, tiled=True)
    packets, summed_all, proj_full = lax.optimization_barrier(
        (packets, summed.astype(BF16), proj_full)
    )
    summed_all = lax.all_gather(summed_all, TENSOR, axis=0, tiled=True)

    share = head_rows // Z
    lines = width // feature_dim // Z
    first = bundle(packets, seq_rows, width // feature_dim, Z)
    first, slot_scores, ge_plane = lax.optimization_barrier((first, slot_scores, ge_plane))
    scores = jnp.sum(jnp.where(placed, slot_scores, 0.0), axis=0)[None, :]
    first = lax.all_to_all(first, "z", 0, 0, tiled=True)
    second = jnp.sum(first.astype(F32), axis=0, keepdims=True).astype(BF16)

    grad_embedded, packets = lax.optimization_barrier((grad_embedded, packets))
    grad_normed = lax.dot_general(
        grad_embedded, head_full, (((1,), (1,)), ((), ())), preferred_element_type=F32
    )
    scaled = grad_normed * norm_gain
    residual_grad = (
        inv_rms * scaled - summed * inv_rms**3 * jnp.mean(summed * scaled, axis=-1, keepdims=True)
    ).astype(BF16)
    ge_all = lax.dynamic_slice_in_dim(ge_plane, here_y * (X * C), X * C, 0)
    ge_all = ge_all.reshape(X * C * seq_rows, feature_dim)
    gained_head = (head_full.astype(F32) * norm_gain[:, None]).astype(BF16)
    mixed_head = jnp.dot(proj_full, gained_head, preferred_element_type=F32).astype(BF16)
    second, mixed_head, residual_grad = lax.optimization_barrier(
        (second, mixed_head, residual_grad)
    )
    second = lax.all_to_all(
        jnp.broadcast_to(second, (Z,) + second.shape[1:]), "z", 0, 0, tiled=True
    )
    pulled = lax.dot_general(
        summed_all, proj_full, (((1,), (1,)), ((), ())), preferred_element_type=F32
    )
    wide = summed_all.astype(F32)
    inv_all = lax.rsqrt(jnp.mean(wide * wide, axis=-1, keepdims=True) + EPS)
    embedded_all = jnp.dot(summed_all, gained_head, preferred_element_type=F32)
    pull_all = jnp.sum(ge_all.astype(F32) * embedded_all, axis=-1, keepdims=True) * (1.0 / width)
    context_grad = (
        inv_all
        * lax.dot_general(
            ge_all, mixed_head, (((1,), (1,)), ((), ())), preferred_element_type=F32
        )
        - inv_all**3 * pull_all * pulled
    ).astype(BF16)

    second, context_grad = lax.optimization_barrier((second, context_grad))
    head_grad = second[:, :share].astype(F32).reshape(head_rows, feature_dim) * gain_blk[:, None]
    gain_grad = second[:, share : share + lines].astype(F32).reshape(width)
    return (scores, context_grad, residual_grad, head_grad, gain_grad)


def solution(mesh):
    split = Mesh(mesh.devices.reshape(Y, Z, X, C), ("y", "z", "x", "c"))
    both = DP + TENSOR
    in_specs = (
        P(both, None),
        P(DP, TENSOR),
        P(TENSOR, DP),
        P(),
        P(TENSOR, None),
        P(both, None),
        P(DP),
        P(DP, None),
        P(DP, None),
        P(),
        P(),
    )
    out_specs = (
        P(both, None),
        P(DP, TENSOR),
        P(both, None),
        P(TENSOR, None),
        P(),
    )
    return jax.shard_map(local, mesh=split, in_specs=in_specs, out_specs=out_specs, check_vma=False)
```

```python
import jax
import jax.numpy as jnp
from jax import lax
from jax.experimental import pallas as pl
from jax.experimental.pallas import tpu as pltpu
from jax.sharding import Mesh, PartitionSpec as P

EPS = 1e-06
TEMPER = 0.1
LOSS_SCALE = 64.0

Y, Z, X, C = 4, 16, 4, 2
DP = ("y", "z")
TENSOR = ("x", "c")
PLANE = ("y", "x", "c")

BF16 = jnp.bfloat16
F32 = jnp.float32
I32 = jnp.int32
VMEM = pl.BlockSpec(memory_space=pltpu.VMEM)
SMEM = pl.BlockSpec(memory_space=pltpu.SMEM)


def swap(values, axis, size, step):
    return lax.ppermute(values, axis, [(i, i ^ step) for i in range(size)])


def rows_of(values, index):
    return values.at[index].get(mode="promise_in_bounds")


def unxor(blocks, place):
    blocks = list(blocks)
    bit = 1
    while bit < len(blocks):
        other = (place & bit) != 0
        blocks = [jnp.where(other, blocks[i ^ bit], block) for i, block in enumerate(blocks)]
        bit *= 2
    return blocks


def decode_kernel(buckets, packed, rows, out):
    words = packed.shape[1]
    features = out.shape[1]
    feature = lax.broadcasted_iota(I32, (words, features), 1)
    word = lax.broadcasted_iota(I32, (words, features), 0)
    here = (feature >> 3) == word
    first = (feature & 7) < 4
    spread_low = jnp.where(here & first, 1.0, 0.0).astype(BF16)
    spread_high = jnp.where(here & ~first, 1.0, 0.0).astype(BF16)
    step = 256
    shift = 2 * (lax.broadcasted_iota(I32, (step, features), 1) & 3)
    zero, one, two, three = [buckets[k] for k in range(4)]

    @pl.loop(0, out.shape[0] // step)
    def _(i):
        at = pl.ds(pl.multiple_of(i * step, step), step)
        codes = packed[at, :]
        code_bytes = jnp.dot(
            (codes & 255).astype(F32).astype(BF16), spread_low, preferred_element_type=F32
        ) + jnp.dot(
            ((codes >> 8) & 255).astype(F32).astype(BF16), spread_high, preferred_element_type=F32
        )
        codes = (code_bytes.astype(I32) >> shift) & 3
        low = (codes & 1).astype(F32)
        high = (codes >> 1).astype(F32)
        levels = zero + low * (one - zero) + high * (two - zero)
        levels = levels + low * high * (three - two - one + zero)
        vectors = rows[at, :].astype(F32) + levels
        scale = lax.rsqrt(jnp.sum(vectors * vectors, axis=1, keepdims=True) + EPS)
        out[at, :] = (vectors * scale).astype(BF16)


def decode_all(cell_ids, packed, centroids, buckets):
    count = cell_ids.size
    packed = packed.reshape(count, packed.size // count)
    rows = rows_of(centroids, cell_ids.reshape(count))
    return pl.pallas_call(
        decode_kernel,
        in_specs=[SMEM, VMEM, VMEM],
        out_specs=VMEM,
        out_shape=jax.ShapeDtypeStruct((count, centroids.shape[1]), BF16),
        compiler_params=pltpu.CompilerParams(vmem_limit_bytes=32 * 1024 * 1024),
        name="decode",
    )(buckets, packed, rows)


def score_kernel(docs, embedded_ref, spans, flags, unit, head, scores, packet, weights, totals):
    slots, queries_n = totals.shape
    tokens = docs.shape[0] // slots
    features = docs.shape[1]
    embedded = embedded_ref[...]
    inverse = lax.rsqrt(jnp.sum(embedded * embedded, axis=1, keepdims=True) + EPS)
    queries = (embedded * inverse).astype(BF16)
    group = 8
    token = lax.broadcasted_iota(I32, (tokens, queries_n), 0)

    @pl.loop(0, slots // group)
    def _(i):
        at = pl.multiple_of(i * (group * tokens), group * tokens)
        slot0 = pl.multiple_of(i * group, group)
        similar = lax.dot_general(
            docs[pl.ds(at, group * tokens), :],
            queries,
            (((1,), (1,)), ((), ())),
            preferred_element_type=F32,
        )
        sizes = spans[pl.ds(slot0, group), :]
        sums = []
        for g in range(group):
            one = jnp.exp(similar[g * tokens : (g + 1) * tokens] / TEMPER)
            one = jnp.where(token < sizes[g : g + 1, :], one, 0.0)
            weights[pl.ds(at + g * tokens, tokens), :] = one
            sums.append(jnp.sum(one, axis=0, keepdims=True))
        totals[pl.ds(slot0, group), :] = jnp.concatenate(sums, axis=0)

    all_totals = totals[...]
    slot_scores = TEMPER * jnp.sum(jnp.log(all_totals), axis=1, keepdims=True)
    scores[...] = slot_scores
    filled = flags[:, 0:1] > 0
    positive = flags[:, 1:2] > 0
    exponent = jnp.where(filled, jnp.exp(slot_scores), 0.0)
    share = exponent / jnp.sum(exponent, axis=0, keepdims=True)
    seeds = LOSS_SCALE * (share - jnp.where(positive, 1.0, 0.0))
    totals[...] = seeds / all_totals

    def add(i, total):
        at = pl.multiple_of(i * (group * tokens), group * tokens)
        slot0 = pl.multiple_of(i * group, group)
        factors = totals[pl.ds(slot0, group), :]
        mixing = [
            weights[pl.ds(at + g * tokens, tokens), :] * factors[g : g + 1, :]
            for g in range(group)
        ]
        mixing = jnp.concatenate(mixing, axis=0).astype(BF16)
        return total + lax.dot_general(
            mixing,
            docs[pl.ds(at, group * tokens), :],
            (((0,), (0,)), ((), ())),
            preferred_element_type=F32,
        )

    grad_q = lax.fori_loop(0, slots // group, add, jnp.zeros((queries_n, features), F32))
    along = jnp.sum(embedded * grad_q, axis=1, keepdims=True)
    grad_embedded = (inverse * grad_q - inverse * inverse * inverse * embedded * along).astype(BF16)
    packet[0:queries_n, :] = grad_embedded

    block = 8
    for i in range(head.shape[0] // (block * features)):
        sums = []
        for k in range(i * block, (i + 1) * block):
            at = slice(k * features, (k + 1) * features)
            grad_normed = lax.dot_general(
                grad_embedded, head[at, :], (((1,), (1,)), ((), ())), preferred_element_type=F32
            )
            sums.append(jnp.sum(grad_normed * unit[:, at], axis=0, keepdims=True))
        line = queries_n + i * block
        packet[line : line + block, :] = jnp.concatenate(sums, axis=0).astype(BF16)


def score(docs, embedded, spans, flags, unit, head):
    slots = flags.shape[0]
    queries_n, features = embedded.shape
    count = docs.shape[0]
    return pl.pallas_call(
        score_kernel,
        in_specs=[VMEM] * 6,
        out_specs=[VMEM] * 2,
        out_shape=[
            jax.ShapeDtypeStruct((slots, 1), F32),
            jax.ShapeDtypeStruct((queries_n + head.shape[0] // features, features), BF16),
        ],
        scratch_shapes=[
            pltpu.VMEM((count, queries_n), F32),
            pltpu.VMEM((slots, queries_n), F32),
        ],
        compiler_params=pltpu.CompilerParams(vmem_limit_bytes=32 * 1024 * 1024),
        cost_estimate=pl.CostEstimate(
            flops=4 * count * queries_n * features,
            bytes_accessed=30_000_000,
            transcendentals=count * queries_n,
        ),
        name="score",
    )(docs, embedded, spans, flags, unit, head)


def bundle_kernel(packets, unit, out, ge):
    count, tall, features = packets.shape
    tokens = unit.shape[0] // count
    shares, _, _ = out.shape
    total = jnp.zeros((tall - tokens, features), F32)
    for i in range(count):
        ge[i * tokens : (i + 1) * tokens, :] = packets[i, 0:tokens, :]
        total = total + packets[i, tokens:tall, :].astype(F32)
    head = lax.dot_general(
        ge[...], unit[...], (((0,), (0,)), ((), ())), preferred_element_type=F32
    ).T
    share = head.shape[0] // shares
    lines = total.shape[0] // shares
    for i in range(shares):
        out[i, 0:share, :] = head[i * share : (i + 1) * share].astype(BF16)
        gain = jnp.concatenate(
            [total[i * lines : (i + 1) * lines], jnp.zeros((16 - lines, features), F32)]
        )
        out[i, share : share + 16, :] = gain.astype(BF16)


def bundle(packets, unit, shares):
    count, tall, features = packets.shape
    return pl.pallas_call(
        bundle_kernel,
        in_specs=[VMEM] * 2,
        out_specs=VMEM,
        out_shape=jax.ShapeDtypeStruct((shares, unit.shape[1] // shares + 16, features), BF16),
        scratch_shapes=[pltpu.VMEM((unit.shape[0], features), BF16)],
        compiler_params=pltpu.CompilerParams(vmem_limit_bytes=32 * 1024 * 1024),
        name="bundle",
    )(packets, unit)


def local(
    residual,
    context,
    out_proj,
    norm_gain,
    colbert_head,
    candidates,
    lengths,
    centroid_ids,
    residual_codes,
    centroids,
    buckets,
):
    shards = Y * Z
    seq_rows, width = residual.shape
    cand_count = candidates.shape[1]
    per_shard, doc_len = centroid_ids.shape
    feature_dim = centroids.shape[1]
    cap = 2
    slots = shards * cap

    slot_ids = candidates.reshape(-1)
    owners = slot_ids // per_shard
    local_ids = slot_ids - owners * per_shard
    order = jnp.arange(cand_count, dtype=I32)
    earlier = (owners[None, :] == owners[:, None]) & (order[None, :] < order[:, None])
    rank = jnp.sum(earlier.astype(I32), axis=1)
    position = owners * cap + rank
    slot_at = jnp.arange(slots, dtype=I32)
    placed = position[None, :] == slot_at[:, None]
    request = jnp.sum(jnp.where(placed, local_ids[None, :], 0), axis=1)
    filled = jnp.any(placed, axis=1)
    flags = jnp.stack([filled, slot_at == position[0]], axis=1).astype(I32)
    note = jnp.concatenate(
        [
            jnp.broadcast_to(lengths[None, :], (shards, per_shard)),
            request.reshape(shards, cap),
            jnp.zeros((shards, 128 - per_shard - cap), I32),
        ],
        axis=1,
    )

    proj_z = lax.all_gather(out_proj, "z", axis=1, tiled=True)
    documents = decode_all(centroid_ids, residual_codes, centroids, buckets)
    notes = lax.all_to_all(note, DP, 0, 0, tiled=True)
    documents = documents.reshape(per_shard, doc_len, feature_dim)
    chosen = rows_of(documents, notes[:, per_shard : per_shard + cap].reshape(slots))
    chosen, colbert_head = lax.optimization_barrier((chosen, colbert_head))
    proj_z, context = lax.optimization_barrier((proj_z, context))
    got_docs = lax.all_to_all(
        chosen.reshape(shards, cap * doc_len, feature_dim), DP, 0, 0, tiled=True
    ).reshape(slots * doc_len, feature_dim)
    spans = jnp.sum(
        jnp.where(
            jnp.arange(per_shard, dtype=I32)[None, None, :]
            == request.reshape(shards, cap)[:, :, None],
            notes[:, None, :per_shard],
            0,
        ),
        axis=2,
    ).reshape(slots, 1)
    spans = jnp.broadcast_to(spans, (slots, seq_rows))

    here_x, here_c, here_y = lax.axis_index("x"), lax.axis_index("c"), lax.axis_index("y")
    blocks = context.reshape(X, C, seq_rows, context.shape[1])
    blocks = jnp.where(here_c == 0, blocks, blocks[:, ::-1])
    blocks = jnp.stack(unxor(blocks, here_x)).transpose(1, 0, 2, 3)
    by_y = jnp.stack([blocks] + [swap(blocks, "y", Y, step) for step in range(1, Y)], axis=2)
    by_y = by_y.reshape(C, X * Y * seq_rows, context.shape[1])

    head_pair = swap(colbert_head, "c", C, 1)
    head_pair = jnp.where(
        here_c == 0,
        jnp.stack([colbert_head, head_pair]),
        jnp.stack([head_pair, colbert_head]),
    )
    head_full = jnp.stack(
        unxor([head_pair] + [swap(head_pair, "x", X, step) for step in range(1, X)], here_x)
    ).reshape(width, feature_dim)
    head_rows = colbert_head.shape[0]
    mine = (here_x * C + here_c) * head_rows
    gain_blk = lax.dynamic_slice_in_dim(norm_gain, mine, head_rows, 0)
    by_y, head_full, proj_z, gain_blk = lax.optimization_barrier(
        (by_y, head_full, proj_z, gain_blk)
    )

    away = jnp.dot(by_y[1], proj_z, preferred_element_type=F32).astype(BF16)
    away = swap(away, "c", C, 1)
    stay = jnp.dot(by_y[0], proj_z, preferred_element_type=F32).astype(BF16)
    stay = lax.optimization_barrier(stay)
    pair = (stay.astype(F32) + away.astype(F32)).reshape(X, Y, seq_rows, width // Y)
    pieces, row = [pair[step].astype(BF16) for step in range(1, X)], pair[0]
    for step in range(1, X):
        row = row + swap(pieces[step - 1], "x", X, step).astype(F32)
    for_y = row.astype(BF16)
    columns = [for_y[0]] + [swap(for_y[step], "y", Y, step) for step in range(1, Y)]
    attended = jnp.concatenate(unxor(columns, here_y), axis=1).astype(F32)
    summed = residual.astype(F32) + attended
    inv_rms = lax.rsqrt(jnp.mean(summed * summed, axis=-1, keepdims=True) + EPS)
    scaled_sum = summed * inv_rms
    normed = (scaled_sum * norm_gain).astype(BF16)
    embedded = jnp.dot(normed, head_full, preferred_element_type=F32)

    unit = scaled_sum.astype(BF16).reshape(seq_rows, X * C, head_rows).transpose(1, 0, 2)
    unit, got_docs = lax.optimization_barrier((unit, got_docs))
    unit_plane = lax.all_to_all(
        jnp.broadcast_to(unit, (Y,) + unit.shape).reshape((-1,) + unit.shape[1:]),
        PLANE,
        0,
        0,
        tiled=True,
    ).reshape(Y * X * C * seq_rows, head_rows)

    slot_scores, packet = score(got_docs, embedded, spans, flags, scaled_sum, head_full)
    packet, unit_plane = lax.optimization_barrier((packet, unit_plane))
    packets = lax.all_to_all(
        jnp.broadcast_to(packet, (Y * X * C,) + packet.shape), PLANE, 0, 0, tiled=True
    )
    ge_plane = packets[:, :seq_rows]

    proj_full = lax.all_gather(proj_z, "y", axis=1, tiled=True)
    packets, summed_all, proj_full = lax.optimization_barrier(
        (packets, summed.astype(BF16), proj_full)
    )
    summed_all = lax.all_gather(summed_all, TENSOR, axis=0, tiled=True)

    share = head_rows // Z
    lines = width // feature_dim // Z
    first = bundle(packets, unit_plane, Z)
    first, slot_scores, ge_plane = lax.optimization_barrier((first, slot_scores, ge_plane))
    scores = jnp.sum(jnp.where(placed, slot_scores, 0.0), axis=0)[None, :]
    first = lax.all_to_all(first, "z", 0, 0, tiled=True)
    second = jnp.sum(first.astype(F32), axis=0, keepdims=True).astype(BF16)
    packet, packets = lax.optimization_barrier((packet, packets))
    grad_embedded = packet[:seq_rows]
    grad_normed = lax.dot_general(
        grad_embedded, head_full, (((1,), (1,)), ((), ())), preferred_element_type=F32
    )
    scaled = grad_normed * norm_gain
    residual_grad = (
        inv_rms * scaled - summed * inv_rms**3 * jnp.mean(summed * scaled, axis=-1, keepdims=True)
    ).astype(BF16)
    ge_all = lax.dynamic_slice_in_dim(ge_plane, here_y * (X * C), X * C, 0)
    ge_all = ge_all.reshape(X * C * seq_rows, feature_dim)
    gained_head = (head_full.astype(F32) * norm_gain[:, None]).astype(BF16)
    mixed_head = jnp.dot(proj_full, gained_head, preferred_element_type=F32).astype(BF16)
    second, mixed_head, residual_grad = lax.optimization_barrier(
        (second, mixed_head, residual_grad)
    )
    second = lax.all_to_all(
        jnp.broadcast_to(second, (Z,) + second.shape[1:]), "z", 0, 0, tiled=True
    )
    pulled = lax.dot_general(
        summed_all, proj_full, (((1,), (1,)), ((), ())), preferred_element_type=F32
    )
    wide = summed_all.astype(F32)
    inv_all = lax.rsqrt(jnp.mean(wide * wide, axis=-1, keepdims=True) + EPS)
    embedded_all = jnp.dot(summed_all, gained_head, preferred_element_type=F32)
    pull_all = jnp.sum(ge_all.astype(F32) * embedded_all, axis=-1, keepdims=True) * (1.0 / width)
    context_grad = (
        inv_all
        * lax.dot_general(
            ge_all, mixed_head, (((1,), (1,)), ((), ())), preferred_element_type=F32
        )
        - inv_all**3 * pull_all * pulled
    ).astype(BF16)

    second, context_grad = lax.optimization_barrier((second, context_grad))
    head_grad = second[:, :share].astype(F32).reshape(head_rows, feature_dim) * gain_blk[:, None]
    gain_grad = second[:, share : share + lines].astype(F32).reshape(width)
    return (scores, context_grad, residual_grad, head_grad, gain_grad)


def solution(mesh):
    split = Mesh(mesh.devices.reshape(Y, Z, X, C), ("y", "z", "x", "c"))
    both = DP + TENSOR
    in_specs = (
        P(both, None),
        P(DP, TENSOR),
        P(TENSOR, DP),
        P(),
        P(TENSOR, None),
        P(both, None),
        P(DP),
        P(DP, None),
        P(DP, None),
        P(),
        P(),
    )
    out_specs = (
        P(both, None),
        P(DP, TENSOR),
        P(both, None),
        P(TENSOR, None),
        P(),
    )
    return jax.shard_map(local, mesh=split, in_specs=in_specs, out_specs=out_specs, check_vma=False)
```
